32 devices in a mesh: dp: 16 (over z, y, core), mp: 2 (over x).
Axes of the slice: x: 2, y: 2, z: 4, core: 2. Of those that a mesh axis runs over, the one named last changes fastest.
Arguments:
- inputs: bfloat16 [128, 1152, 256], P('dp', 'mp'), may hold values from -6 to 6
- condition: bfloat16 [128, 1152], P('dp', 'mp'), may hold values from -6 to 6
- cotangent: bfloat16 [128, 1152, 256], P('dp', 'mp'), may hold values from -6 to 6
- kept_rows: int32 [128, 192], P('dp'), may hold values from 0 to 255, as said below
- kept_counts: int32 [128], P('dp'), may hold values from 64 to 192, as said below
- group_tokens: int32 [128], P('dp'), may hold values from 64 to 285, as said below
- w_qkv: bfloat16 [1152, 3, 1152], P('dp', None, 'mp'), may hold values from -0.1875 to 0.1875
- b_qv: bfloat16 [2, 1152], P(None, 'mp'), may hold values from -3 to 3
- w_out: bfloat16 [1152, 1152], P('mp', 'dp'), may hold values from -0.75 to 0.75
- b_out: bfloat16 [1152], P('mp'), may hold values from -3 to 3
- w_one: bfloat16 [1152, 4608], P('dp', 'mp'), may hold values from -0.1875 to 0.1875
- b_one: bfloat16 [4608], P('mp'), may hold values from -3 to 3
- w_two: bfloat16 [4608, 1152], P('mp', 'dp'), may hold values from -0.09375 to 0.09375
- b_two: bfloat16 [1152], P('mp'), may hold values from -3 to 3
- w_ada: bfloat16 [1152, 6, 1152], P('dp', None, 'mp'), may hold values from -0.1875 to 0.1875
- b_ada: bfloat16 [6, 1152], P(None, 'mp'), may hold values from -3 to 3
Outputs:
- output: bfloat16 [128, 1152, 256], P('dp', 'mp')
- input_grad: float32 [128, 1152, 256], P('dp', 'mp')
- cond_grad: float32 [128, 1152], P('dp', 'mp')
- grad_w_qkv: float32 [1152, 3, 1152], P('dp', None, 'mp')
- gradient_query_value_bias: float32 [2, 1152], P(None, 'mp')
- grad_w_out: float32 [1152, 1152], P('mp', 'dp')
- grad_b_out: float32 [1152], P('mp')
- grad_w_one: float32 [1152, 4608], P('dp', 'mp')
- grad_b_one: float32 [4608], P('mp')
- grad_w_two: float32 [4608, 1152], P('mp', 'dp')
- grad_b_two: float32 [1152], P('mp')
- gradient_adaptive_weight: float32 [1152, 6, 1152], P('dp', None, 'mp')
- grad_b_ada: float32 [6, 1152], P(None, 'mp')
The draws below stay inside these ranges and needn't reach their ends.
Inputs may be any that keep to these rules, and one draw needn't show every extreme that they name: `kept_rows`: for latent l the first kept_counts[l] entries are the kept rows in increasing order; all entries of a latent are distinct. `kept_counts`: some latent keeps 192 tokens and some keeps 192 // 3. `group_tokens`: positive counts.
All inputs are finite; a program needn't handle non-finite values.
Results may differ from the reference program's by a relative error of at most 0.012.
The reference program's roundings to bfloat16 on the way count: a program that leaves them out, or rounds other values in their place, can miss the bound.
Values may be sent and summed in bfloat16 or wider, within the bound.
No kernel may reach another device: no remote copies, remote signals or barrier semaphores. Data moves between devices by JAX's collectives and lax.ppermute only.
A program may use at most 320 MiB of HBM per device.

```python
import math
import jax
import jax.numpy as jnp
from jax import lax

D = 1152
HEADS = 16
HD = 72
FF = 4608
S = 256
KEEP = 192
LAT_DEV = 8
LAT = 128


def kept_layout(key):
    count_key, first_key, second_key, order_key = jax.random.split(key, 4)
    counts = jax.random.randint(count_key, (LAT,), KEEP // 3, KEEP + 1)
    top_at = jax.random.randint(first_key, (), 0, LAT)
    low_at = (top_at + 1 + jax.random.randint(second_key, (), 0, LAT - 1)) % LAT
    counts = counts.at[top_at].set(KEEP).at[low_at].set(KEEP // 3)
    orders = jax.vmap(lambda sub_key: jax.random.permutation(sub_key, S))(jax.random.split(order_key, LAT))
    slot_ids = jnp.arange(S)[None, :]
    marked = jnp.where(slot_ids < counts[:, None], orders, S + orders)
    ranked = jnp.sort(marked, axis=1)[:, :KEEP]
    chosen = jnp.where(ranked >= S, ranked - S, ranked)
    return (chosen.astype(jnp.int32), counts.astype(jnp.int32))


def draw_kept_rows(key, part):
    rows_drawn, counts_drawn = kept_layout(key)
    return rows_drawn


def draw_kept_counts(key, part):
    rows_drawn, counts_drawn = kept_layout(key)
    return counts_drawn


def draw_group_tokens(key, part):
    key = jax.random.fold_in(key, 5)
    noise = jax.random.randint(key, (LAT,), 0, 32)
    noise = noise.at[0].set(0).at[LAT - 1].set(31)
    return (64 + noise + 192 * jnp.arange(LAT) // LAT).astype(jnp.int32)


def levels(key, dims, cuts, smallest, top_value):
    level, own = 1.0, jax.random.fold_in(key, 6)
    for dim, shards_of in cuts:
        heights = jnp.exp(jax.random.uniform(jax.random.fold_in(own, dim), (shards_of,), jnp.float32, smallest / len(cuts), top_value / len(cuts)))
        level = level * jnp.repeat(heights, dims[dim] // shards_of).reshape([-1 if axis == dim else 1 for axis in range(len(dims))])
    return level


def normal_values(key, dims, scale, bound, cuts=(), dtype=jnp.bfloat16):
    loudness = levels(key, dims, cuts, -0.22, 0.18) if cuts else 1.0
    values = jax.random.normal(key, dims, jnp.float32) * scale * loudness
    return jnp.minimum(jnp.maximum(values, -bound), bound).astype(dtype)


def setup_inputs(seed: int = 0) -> dict:
    keys = jax.random.split(jax.random.key(seed), 17)
    inputs = normal_values(keys[0], (LAT, D, S), 1.0, 6.0, ((0, 16), (1, 2)))
    condition = normal_values(keys[1], (LAT, D), 1.0, 6.0, ((0, 16), (1, 2)))
    cotangent = normal_values(keys[2], (LAT, D, S), 1.0, 6.0, ((0, 16), (1, 2)))
    kept_rows = draw_kept_rows(jax.random.fold_in(keys[16], 71), 0)
    kept_counts = draw_kept_counts(jax.random.fold_in(keys[16], 71), 0)
    group_tokens = draw_group_tokens(jax.random.fold_in(keys[16], 71), 0)
    w_qkv = normal_values(keys[6], (D, 3, D), D ** -0.5, 0.1875, ((0, 16), (2, 2)))
    b_qv = normal_values(keys[7], (2, D), 0.5, 3.0, ((1, 2),))
    w_out = normal_values(keys[8], (D, D), HD ** -0.5, 0.75, ((0, 2), (1, 16)))
    b_out = normal_values(keys[9], (D,), 0.5, 3.0, ((0, 2),))
    w_one = normal_values(keys[10], (D, FF), D ** -0.5, 0.1875, ((0, 16), (1, 2)))
    b_one = normal_values(keys[11], (FF,), 0.5, 3.0, ((0, 2),))
    w_two = normal_values(keys[12], (FF, D), FF ** -0.5, 0.09375, ((0, 2), (1, 16)))
    b_two = normal_values(keys[13], (D,), 0.5, 3.0, ((0, 2),))
    w_ada = normal_values(keys[14], (D, 6, D), D ** -0.5, 0.1875, ((0, 16), (2, 2)))
    b_ada = normal_values(keys[15], (6, D), 0.5, 3.0, ((1, 2),))
    return dict(inputs=inputs, condition=condition, cotangent=cotangent, kept_rows=kept_rows, kept_counts=kept_counts, group_tokens=group_tokens, w_qkv=w_qkv, b_qv=b_qv, w_out=w_out, b_out=b_out, w_one=w_one, b_one=b_one, w_two=w_two, b_two=b_two, w_ada=w_ada, b_ada=b_ada)


@jax.custom_vjp
def low(v):
    return lax.optimization_barrier(v.astype(jnp.bfloat16)).astype(jnp.float32)

@jax.custom_vjp
def low_back(v):
    return v

def low_keep(v):
    return (low(v), None)

def low_pass(kept, grad):
    return (grad,)

def back_keep(v):
    return (v, None)

def back_low(kept, grad):
    return (low(grad),)
low.defvjp(low_keep, low_pass)
low_back.defvjp(back_keep, back_low)
EPS = 1e-06
HIGH = lax.Precision.HIGHEST

def matmul(left, right):
    return jnp.dot(left, right, precision=HIGH, preferred_element_type=jnp.float32)

def norm_rows(values):
    center = lax.optimization_barrier(jnp.mean(values, axis=-1, keepdims=True))
    spread = lax.optimization_barrier(jnp.mean(values * values, axis=-1, keepdims=True)) - center * center
    return (values - center) * lax.rsqrt(spread + EPS)

def layer_rows(group_x, group_c, params, slot_rows, slot_counts):
    w_qkv, b_qv, w_out, b_out, w_one, b_one, w_two, b_two, w_ada, b_ada = params
    group_size = group_x.shape[0]
    inv_root = 1.0 / math.sqrt(HD)
    silu_reduced_precision = low(jax.nn.silu(group_c))
    modulation = low_back(matmul(silu_reduced_precision, w_ada.reshape(D, 6 * D)).reshape(group_size, 6, D) + b_ada)
    shift_one, scale_one, first_gate_value, shift_two, scale_two, gate_two = [modulation[:, position, None, :] for position in range(6)]
    kept_slot = jax.vmap(lambda table_rows, places: table_rows[places])(group_x, slot_rows)
    is_valid = jnp.arange(KEEP)[None, :] < slot_counts[:, None]
    first_in = low(norm_rows(kept_slot) * (1.0 + scale_one) + shift_one)
    projected = matmul(first_in.reshape(-1, D), w_qkv.reshape(D, 3 * D)).reshape(group_size, KEEP, 3, HEADS, HD)
    queries = low(low_back(projected[:, :, 0] + b_qv[0].reshape(HEADS, HD)))
    key_rows = low(low_back(projected[:, :, 1]))
    value_rows = low(low_back(projected[:, :, 2] + b_qv[1].reshape(HEADS, HD)))
    scores = low_back(jnp.einsum('gqhe,gkhe->ghqk', queries, key_rows, precision=HIGH) * inv_root)
    scores = jnp.where(is_valid[:, None, None, :], scores, -1e+30)
    probability = low(jax.nn.softmax(scores, axis=-1))
    mixture = low(low_back(jnp.einsum('ghqk,gkhe->gqhe', probability, value_rows, precision=HIGH)))
    attended = low_back(matmul(mixture.reshape(-1, D), w_out) + b_out).reshape(group_size, KEEP, D)
    residual = kept_slot + first_gate_value * attended
    second_in = low(norm_rows(residual) * (1.0 + scale_two) + shift_two)
    hidden = low_back(matmul(second_in.reshape(-1, D), w_one) + b_one)
    activated = low(jax.nn.gelu(hidden, approximate=True))
    branch = low_back(matmul(activated, w_two) + b_two).reshape(group_size, KEEP, D)
    result = residual + gate_two * branch
    fresh_rows = jnp.where(is_valid[:, :, None], result, kept_slot)
    return jax.vmap(lambda table_rows, places, new_rows: table_rows.at[places].set(new_rows))(group_x, slot_rows, fresh_rows)

def reference(inputs, condition, cotangent, kept_rows, kept_counts, group_tokens, w_qkv, b_qv, w_out, b_out, w_one, b_one, w_two, b_two, w_ada, b_ada):
    token_rows = jnp.swapaxes(inputs, 1, 2)
    cot_rows_all = jnp.swapaxes(cotangent, 1, 2)
    token_total = jnp.sum(group_tokens).astype(jnp.float32)
    row_scale = LAT * group_tokens.astype(jnp.float32) / token_total
    params = tuple((weight_item.astype(jnp.float32) for weight_item in (w_qkv, b_qv, w_out, b_out, w_one, b_one, w_two, b_two, w_ada, b_ada)))
    groups = LAT // LAT_DEV

    def regroup(array_in):
        return array_in.reshape((groups, LAT_DEV) + array_in.shape[1:])

    def scan_step(accumulated, element):
        group_x, group_c, group_t, slot_rows, slot_counts, group_scale = element

        def forward(layer_x, layer_c, layer_params):
            return layer_rows(layer_x, layer_c, layer_params, slot_rows, slot_counts)
        produced, backward = jax.vjp(forward, group_x.astype(jnp.float32), group_c.astype(jnp.float32), params)
        grad_x, grad_c, grad_params = backward(group_t.astype(jnp.float32) * group_scale[:, None, None])
        accumulated = jax.tree.map(lambda total_sum, fresh_term: total_sum + fresh_term, accumulated, grad_params)
        return (accumulated, (produced.astype(jnp.bfloat16), grad_x, grad_c))
    zero_grads = jax.tree.map(jnp.zeros_like, params)
    scanned = (regroup(token_rows), regroup(condition), regroup(cot_rows_all), regroup(kept_rows), regroup(kept_counts), regroup(row_scale))
    summed, stacked = lax.scan(scan_step, zero_grads, scanned)
    output = jnp.swapaxes(stacked[0].reshape(LAT, S, D), 1, 2)
    input_grad = jnp.swapaxes(stacked[1].reshape(LAT, S, D), 1, 2)
    cond_grad = stacked[2].reshape(LAT, D)
    return (output, input_grad, cond_grad, summed[0], summed[1], summed[2], summed[3], summed[4], summed[5], summed[6], summed[7], summed[8], summed[9])
```

```python
from functools import partial
import math

import jax
import jax.numpy as jnp
from jax import lax
from jax.experimental import pallas as pl
from jax.experimental.pallas import tpu as pltpu
from jax.sharding import PartitionSpec as P

HD = 72
EPS = 1e-06
BF = jnp.bfloat16
F32 = jnp.float32
NN = ((1,), (0,))
NT = ((1,), (1,))
TN = ((0,), (0,))


def dot(left, right, dims, kind=F32):
    return lax.dot_general(left, right, (dims, ((), ())), preferred_element_type=kind)


def exact_dot(left, right, dims):
    return lax.dot_general(
        left,
        right,
        (dims, ((), ())),
        precision=lax.Precision.HIGHEST,
        preferred_element_type=F32,
    )


class Steps:
    def __init__(self):
        self.seen = ()

    def __call__(self, *values):
        out = lax.optimization_barrier((*values, *self.seen))[: len(values)]
        self.seen = out
        return out[0] if len(values) == 1 else out


def attend_kernel(heads, counts, qkv_ref, out_ref):
    count = counts[pl.program_id(0)]
    keep, own = out_ref.shape
    inv_root = 1.0 / math.sqrt(HD)
    valid = lax.broadcasted_iota(jnp.int32, (keep, keep), 1) < count
    for h in range(heads):
        a = HD * h
        q, k = qkv_ref[:, a : a + HD], qkv_ref[:, own + a : own + a + HD]
        v = qkv_ref[:, 2 * own + a : 2 * own + a + HD]
        scores = jnp.where(valid, dot(q, k, NT) * inv_root, -1e30)
        power = jnp.exp(scores - jnp.max(scores, axis=1, keepdims=True))
        probability = power / jnp.sum(power, axis=1, keepdims=True)
        out_ref[:, a : a + HD] = dot(probability.astype(BF), v, NN).astype(BF)


def attend_back_kernel(heads, counts, qkv_ref, g_ref, out_ref):
    count = counts[pl.program_id(0)]
    keep, own = g_ref.shape
    inv_root = 1.0 / math.sqrt(HD)
    valid = lax.broadcasted_iota(jnp.int32, (keep, keep), 0) < count
    for h in range(heads):
        a = HD * h
        q, k = qkv_ref[:, a : a + HD], qkv_ref[:, own + a : own + a + HD]
        v, g = qkv_ref[:, 2 * own + a : 2 * own + a + HD], g_ref[:, a : a + HD]
        scores = jnp.where(valid, dot(k, q, NT) * inv_root, -1e30)
        power = jnp.exp(scores - jnp.max(scores, axis=0, keepdims=True))
        probability = power / jnp.sum(power, axis=0, keepdims=True)
        grad_prob = dot(v, g, NT)
        delta = jnp.sum(grad_prob * probability, axis=0, keepdims=True)
        grad_scores = (probability * (grad_prob - delta)).astype(BF)
        out_ref[:, a : a + HD] = (dot(grad_scores, k, TN) * inv_root).astype(BF)
        out_ref[:, own + a : own + a + HD] = (dot(grad_scores, q, NN) * inv_root).astype(BF)
        out_ref[:, 2 * own + a : 2 * own + a + HD] = dot(probability.astype(BF), g, NN).astype(
            BF
        )


def attend(counts, qkv, keep):
    rows, own = qkv.shape[0], qkv.shape[1] // 3

    def block(n):
        return pl.BlockSpec((keep, n), lambda i, c: (i, 0))

    return pl.pallas_call(
        partial(attend_kernel, own // HD),
        out_shape=jax.ShapeDtypeStruct((rows, own), BF),
        grid_spec=pltpu.PrefetchScalarGridSpec(
            num_scalar_prefetch=1,
            grid=(rows // keep,),
            in_specs=[block(3 * own)],
            out_specs=block(own),
        ),
        compiler_params=pltpu.CompilerParams(vmem_limit_bytes=40 * 2**20),
    )(counts, qkv)


def attend_back(counts, qkv, g, keep):
    rows, own = g.shape

    def block(n):
        return pl.BlockSpec((keep, n), lambda i, c: (i, 0))

    return pl.pallas_call(
        partial(attend_back_kernel, own // HD),
        out_shape=jax.ShapeDtypeStruct((rows, 3 * own), BF),
        grid_spec=pltpu.PrefetchScalarGridSpec(
            num_scalar_prefetch=1,
            grid=(rows // keep,),
            in_specs=[block(3 * own), block(own)],
            out_specs=block(3 * own),
        ),
        compiler_params=pltpu.CompilerParams(vmem_limit_bytes=40 * 2**20),
    )(counts, qkv, g)


def local(
    inputs,
    condition,
    cotangent,
    kept_rows,
    kept_counts,
    group_tokens,
    w_qkv,
    b_qv,
    w_out,
    b_out,
    w_one,
    b_one,
    w_two,
    b_two,
    w_ada,
    b_ada,
):
    nd, nm = lax.axis_size("dp"), lax.axis_size("mp")
    d, m = lax.axis_index("dp"), lax.axis_index("mp")
    lat_dev, own, seq = inputs.shape
    keep = kept_rows.shape[1]
    full = own * nm
    blk, nb = full // nd, nd // nm
    mine = lat_dev // nm
    rows = mine * keep
    ff = w_one.shape[1]
    half = full // 2
    far_bits = [b for b in reversed(range(2, nd.bit_length() - 1))]
    bits = far_bits + [1, 0]
    zb = 2 ** len(far_bits)
    shifts = range(nm)

    def over_dp(v, bit):
        return lax.ppermute(v, "dp", [(i, i ^ (1 << bit)) for i in range(nd)])

    def over_mp(v, s):
        return v if s == 0 else lax.ppermute(v, "mp", [(i, i ^ s) for i in range(nm)])

    def rel(place):
        out = jnp.zeros_like(place)
        for k, bit in enumerate(bits):
            out = out | (((place >> k) & 1) << bit)
        return out

    def block_of(place):
        near = place // zb
        return ((place % zb) << 2) | ((d & 3) ^ (((near & 1) << 1) | (near >> 1)))

    def spread(s, kind):
        place = lax.broadcasted_iota(jnp.int32, (own, full), 1)
        feature = lax.broadcasted_iota(jnp.int32, (own, full), 0)
        source = block_of(place // blk)
        wanted = (m ^ s) * nb + feature // blk
        return ((source == wanted) & (place % blk == feature % blk)).astype(kind)

    spreads = [spread(s, BF) for s in shifts]
    place_hot = (
        (d ^ rel(lax.broadcasted_iota(jnp.int32, (nd, nd), 0)))
        == lax.broadcasted_iota(jnp.int32, (nd, nd), 1)
    )
    far_groups = [[low + 4 * k for k in range(zb)] for low in range(4)]
    step = Steps()

    def group_of(v, s):
        return lax.dynamic_slice_in_dim(v, (m ^ s) * mine, mine, 0)

    def regroup(parts):
        stacked = jnp.stack(parts)
        return jnp.concatenate(
            [lax.dynamic_index_in_dim(stacked, m ^ g, 0, keepdims=False) for g in shifts]
        )

    def send_rows(v):
        return [over_mp(group_of(v, s), s).reshape(rows, own) for s in shifts]

    def to_rows(got):
        return sum(dot(g, p, NN) for g, p in zip(got, spreads))

    def from_rows(v):
        parts = [dot(v, p, NT, BF).reshape(mine, keep, own) for p in spreads]
        return [over_mp(part, s) for s, part in enumerate(parts)]

    def far_gather(v):
        return lax.all_gather(v, "dp", axis=0, tiled=True, axis_index_groups=far_groups)

    cond_halves = [over_mp(condition, s) for s in shifts]
    bias_vec = jnp.concatenate([b_qv.reshape(-1), b_one, b_out, b_two])
    bias_all = [over_mp(bias_vec, s) for s in shifts]
    w_a = jnp.concatenate([w_qkv.reshape(blk, 3 * own), w_out.T], axis=1)
    a_z = far_gather(w_a)
    one_z = far_gather(w_one)
    digits = jnp.stack([(group_tokens >> (8 * k)) & 255 for k in range(4)], axis=1)
    pad = -(blk + 4) % 8
    valid = jnp.arange(keep)[None, :] < kept_counts[:, None]
    hot = (
        (kept_rows[:, :, None] == jnp.arange(seq)[None, None, :]) & valid[:, :, None]
    ).astype(BF)

    def pick(source):
        return lax.dot_general(
            hot, source, (((2,), (2,)), ((0,), (0,))), preferred_element_type=BF
        )

    w_a = step(w_a)
    picked = pick(step(inputs))
    picked = step(picked)
    kept_got = send_rows(picked)
    cond_halves = [cond_halves[0], *[step(v) for v in cond_halves[1:]]]
    cond_halves = jnp.stack(cond_halves)
    cond_full = jnp.concatenate(
        [lax.dynamic_index_in_dim(cond_halves, m ^ g, 0, keepdims=False) for g in shifts], axis=1
    )
    cond_send = jnp.concatenate(
        [
            jnp.swapaxes(cond_full.reshape(lat_dev, nd, blk), 0, 1),
            jnp.broadcast_to(digits.astype(BF)[None], (nd, lat_dev, 4)),
            jnp.zeros((nd, lat_dev, pad), BF),
        ],
        axis=2,
    )
    cond_got = lax.all_to_all(cond_send, "dp", 0, 0)
    w_two_t = w_two.T
    w_ada_flat = w_ada.reshape(blk, 6 * own)
    two_z = far_gather(w_two_t)
    w_two_t, w_ada_flat, cond_got = step(w_two_t, w_ada_flat, cond_got)
    cond_got = dot(place_hot.astype(BF), cond_got.reshape(nd, -1), NN).reshape(
        nd, lat_dev, blk + 4 + pad
    )
    token_total = sum(
        jnp.sum(cond_got[:, :, blk + k]) * float(256**k) for k in range(4)
    )
    silu_low = jax.nn.silu(cond_got[:, :, :blk].reshape(nd * lat_dev, blk)).astype(BF)
    part = dot(silu_low, w_ada_flat, NN).reshape(nd, lat_dev, 6 * own)
    part = step(part)

    def part_send(part, bit):
        return over_dp(part[part.shape[0] // 2 :], bit)

    def part_add(part, got):
        return part[: part.shape[0] // 2] + got

    got = part_send(part, 0)
    part = part_add(part, step(got))
    got = part_send(part, 1)

    def core_pair(v):
        return (v, over_dp(v, 0))

    def near_join(a, b):
        return jnp.concatenate([a, b], 0)

    def join(pair, start, stop):
        return jnp.concatenate([v[:, :, start:stop] for v in pair], 0).reshape(full, stop - start)

    def later(vs):
        return [vs[0], *[step(v) for v in vs[1:]]]

    a_z = step(a_z).reshape(zb, blk, 4 * own)
    a_xs = [over_mp(a_z, s) for s in shifts]
    a_y = over_dp(a_z, 1)
    kept_got = later(kept_got)
    kept_slot = step(to_rows(kept_got)).reshape(mine, keep, full)
    part = part_add(part, step(got))
    for bit in reversed(far_bits):
        got = part_send(part, bit)
        part = part_add(part, step(got))
    modulation = part.reshape(lat_dev, 6, own) + b_ada.astype(F32)
    modulation = step(modulation)
    mod_got = [over_mp(group_of(modulation, s), s).reshape(mine * 6, own) for s in shifts]
    a_xs = later(a_xs)
    a_y = step(a_y)
    a_xys = [over_mp(a_y, s) for s in shifts]
    one_z = step(one_z).reshape(zb, blk, ff)
    one_y = over_dp(one_z, 1)
    a_pairs = {0: core_pair(step(near_join(a_z, a_y)))}
    mod_got = later(mod_got)
    mod_rows = sum(
        exact_dot(v, p.astype(F32), NN) for v, p in zip(mod_got, spreads)
    ).reshape(mine, 6, full)
    shift_one, scale_one, gate_one, shift_two, scale_two, gate_two = [
        mod_rows[:, k, None, :] for k in range(6)
    ]
    bias_qv = [v[: 2 * own].reshape(2, own).astype(F32) for v in bias_all]
    bias_one = [v[2 * own : 2 * own + ff].astype(F32) for v in bias_all]
    bias_wide = sum(
        dot(v[2 * own + ff :].reshape(2, own), p, NN) for v, p in zip(bias_all, spreads)
    )
    row_scale = lat_dev * nd * group_tokens.astype(F32) / token_total
    own_scale = group_of(row_scale, 0)[:, None, None]
    own_counts = group_of(kept_counts, 0)

    def cubes(v):
        return v.reshape(mine, keep, -1)

    def flat(v):
        return v.reshape(rows, -1)

    def column_sums(v):
        return dot(jnp.ones((8, rows), BF), v, NN)[0]

    def normalize(v):
        center = jnp.mean(v, axis=-1, keepdims=True)
        var = jnp.mean(v * v, axis=-1, keepdims=True) - center * center
        scaled = lax.rsqrt(var + EPS)
        return (v - center) * scaled, scaled

    def norm_back(g, normed, scaled):
        a = jnp.mean(g, axis=-1, keepdims=True)
        b = jnp.mean(g * normed, axis=-1, keepdims=True)
        return (g - a - normed * b) * scaled

    normed_one, scaled_one = normalize(kept_slot)
    first_low = flat((normed_one * (1.0 + scale_one) + shift_one).astype(BF))
    first_low = step(first_low)
    w_qkvs, wo_t, qkvs, mixtures = [], [], [], []
    attended = bias_wide[0]
    for s in shifts:
        pair = (a_pairs[s][0], step(a_pairs[s][1]))
        w_qkvs.append(join(pair, 0, 3 * own))
        wo_t.append(join(pair, 3 * own, 4 * own))
        bias = jnp.concatenate([bias_qv[s][0], jnp.zeros((own,), F32), bias_qv[s][1]])
        qkv = step((dot(first_low, w_qkvs[s], NN) + bias).astype(BF))
        qkvs.append(qkv)
        mixture = step(attend(own_counts, qkv, keep))
        mixtures.append(mixture)
        attended = step(attended + dot(mixture, wo_t[s], NT))
        if s == 0:
            a_xys = later(a_xys)
            one_y = step(one_y)
            one_xs = [over_mp(one_z, t) for t in shifts]
            two_z = step(two_z).reshape(zb, blk, ff)
            two_y = over_dp(two_z, 1)
            for t in shifts[1:]:
                a_pairs[t] = core_pair(step(near_join(a_xs[t], a_xys[t])))
            g_one = {0: core_pair(step(near_join(one_z, one_y)))}
    one_xs = later(one_xs)
    two_y = step(two_y)
    two_xs = [over_mp(two_z, s) for s in shifts]
    one_xys = [one_y, *[over_dp(v, 1) for v in one_xs[1:]]]
    g_two = {0: core_pair(step(near_join(two_z, two_y)))}
    attended = cubes(attended)
    residual = kept_slot + gate_one * attended
    normed_two, scaled_two = normalize(residual)
    second_low = flat((normed_two * (1.0 + scale_two) + shift_two).astype(BF))
    second_low = step(second_low)
    branch = bias_wide[1]
    w1, w2t, acts, slopes = [], [], [], []
    root = math.sqrt(2.0 / math.pi)
    for s in shifts:
        w1.append(join((g_one[s][0], step(g_one[s][1])), 0, ff))
        hidden = dot(second_low, w1[s], NN) + bias_one[s]
        square = hidden * hidden
        bend = jnp.tanh(root * hidden * (1.0 + 0.044715 * square))
        act = (0.5 * hidden * (1.0 + bend)).astype(BF)
        slope = 0.5 * (1.0 + bend) + 0.5 * root * hidden * (1.0 - bend * bend) * (
            1.0 + 3.0 * 0.044715 * square
        )
        act, slope = step(act, slope)
        acts.append(act)
        slopes.append(slope)
        if s == 0:
            two_xs = later(two_xs)
            one_xys = later(one_xys)
            two_xys = [over_mp(two_y, t) for t in shifts]
            for t in shifts[1:]:
                g_one[t] = core_pair(step(near_join(one_xs[t], one_xys[t])))
            mixture_all = jnp.concatenate(mixtures, axis=1)
            cot_picked = step(pick(cotangent))
        if s:
            for t in shifts[1:]:
                two_xys[t] = step(two_xys[t]) if s == 1 else two_xys[t]
            if s == 1:
                cot_got = send_rows(cot_picked)
            g_two[s] = core_pair(step(near_join(two_xs[s], two_xys[s])))
        w2t.append(join((g_two[s][0], step(g_two[s][1])), 0, ff))
        branch = step(branch + dot(act, w2t[s], NT))
    branch = cubes(branch)
    result = residual + gate_two * branch
    cot_got = later(cot_got)
    fresh_got = from_rows(flat(result).astype(BF))

    def add(a, b):
        return (a.astype(F32) + b.astype(F32)).astype(BF)

    def keep_sum(low_side, v, got):
        kept = (dot(low_side, v, TN) + got.astype(F32)).astype(BF)
        return kept.reshape(2 * zb, blk, -1)

    def y_send(v):
        return over_dp(v[zb:], 1)

    def y_add(v, got):
        return add(v[:zb], got)

    def x_send(vs):
        return {s: over_mp(v, s) for s, v in vs.items() if s}

    def x_add(vs, got):
        total = vs[0].astype(F32)
        for v in got:
            total = total + v.astype(F32)
        return total.astype(BF)

    cot_rows = to_rows(cot_got).reshape(mine, keep, full)
    grad_result = cot_rows * own_scale
    grad_branch = flat((gate_two * grad_result).astype(BF))
    order = list(reversed(shifts))

    def far_scatter(v):
        v = v.reshape(zb * blk, -1)
        v = lax.psum_scatter(
            v, "dp", scatter_dimension=0, tiled=True, axis_index_groups=far_groups
        )
        return v.astype(F32)

    low, high, grad_branch = step(grad_branch[:, :half], grad_branch[:, half:], grad_branch)
    two_sent, two_got, two_kept, two_y_got, two_y, two_x_got = {}, {}, {}, {}, {}, {}
    grad_hiddens = [None] * nm
    for s in order:
        two_sent[s] = step(dot(high, acts[s], TN, BF))
        two_got[s] = over_dp(two_sent[s], 0)
    for s in order:
        grad_hiddens[s] = step((dot(step(grad_branch), w2t[s], NN) * slopes[s]).astype(BF))
        two_kept[s] = step(keep_sum(low, acts[s], step(two_got[s])))
        two_y_got[s] = y_send(two_kept[s])
    low, high = step(second_low[:, :half], second_low[:, half:])
    one_sent, one_got, one_kept = {}, {}, {}
    for s in order:
        one_sent[s] = step(dot(high, grad_hiddens[s], TN, BF))
        one_got[s] = over_dp(one_sent[s], 0)
    fresh_got = later(fresh_got)
    last = order[0]
    grad_second = step(
        sum(dot(v, w, NT) for v, w in zip(lax.optimization_barrier(grad_hiddens), w1))
    )
    one_x_got = {}
    for s in order:
        one_kept[s] = step(keep_sum(low, grad_hiddens[s], step(one_got[s])))
        if s:
            one_x_got[s] = (over_mp(one_kept[s][zb:], s), over_mp(one_kept[s][:zb], s))
    grad_second = cubes(step(grad_second))
    grad_shift_two = jnp.sum(grad_second, axis=1)
    grad_scale_two = jnp.sum(grad_second * normed_two, axis=1)
    grad_residual = grad_result + norm_back(
        grad_second * (1.0 + scale_two), normed_two, scaled_two
    )
    grad_attended = flat((gate_one * grad_residual).astype(BF))
    low, high, grad_attended = step(
        grad_attended[:, :half], grad_attended[:, half:], grad_attended
    )
    out_sent = step(dot(high, mixture_all, TN, BF))
    out_got = over_dp(out_sent, 0)
    grad_mixtures = step(*[dot(step(grad_attended), w, NN, BF) for w in wo_t])
    out_kept = step(keep_sum(low, mixture_all, step(out_got)))
    for s in order:
        two_y[s] = step(y_add(two_kept[s], step(two_y_got[s])))
    one_high = step(x_add([one_kept[0][zb:]], [step(v[0]) for v in one_x_got.values()]))
    one_y_got = over_dp(one_high, 1)
    two_x_got = x_send(two_y)
    grad_qkvs = [None] * nm
    first_half, second_half = step(first_low[:, :half], first_low[:, half:])
    qkv_sent, qkv_got, qkv_kept, qkv_y_got, qkv_y = {}, {}, {}, {}, {}
    for s in order:
        grad_qkvs[s] = step(attend_back(step(own_counts), qkvs[s], grad_mixtures[s], keep))
        if s == last:
            out_y_got = y_send(out_kept)
        qkv_sent[s] = step(dot(second_half, grad_qkvs[s], TN, BF))
        qkv_got[s] = over_dp(qkv_sent[s], 0)
    one_low = step(x_add([one_kept[0][:zb]], [step(v[1]) for v in one_x_got.values()]))
    for s in order:
        qkv_kept[s] = step(keep_sum(first_half, grad_qkvs[s], step(qkv_got[s])))
        qkv_y_got[s] = y_send(qkv_kept[s])
    grad_first = step(
        sum(dot(a, w, NT) for a, w in zip(lax.optimization_barrier(grad_qkvs), w_qkvs))
    )
    two_x = step(x_add(two_y, [step(v) for v in two_x_got.values()]))
    sum_two = far_scatter(two_x)
    out_y = step(y_add(out_kept, step(out_y_got)))
    out_x_got = [over_mp(out_y[:, :, s * own : (s + 1) * own], s) for s in shifts[1:]]
    one_y = step(add(one_low, step(one_y_got)))
    sum_one = far_scatter(one_y)
    grad_first = cubes(step(grad_first))
    grad_shift_one = jnp.sum(grad_first, axis=1)
    grad_scale_one = jnp.sum(grad_first * normed_one, axis=1)
    grad_kept = grad_residual + norm_back(
        grad_first * (1.0 + scale_one), normed_one, scaled_one
    )
    grad_low = step(flat(grad_kept).astype(BF))
    grad_got = from_rows(grad_low)
    grad_gate_two = jnp.sum(grad_result * branch, axis=1)
    grad_gate_one = jnp.sum(grad_residual * attended, axis=1)
    for s in order:
        qkv_y[s] = step(y_add(qkv_kept[s], step(qkv_y_got[s])))
        if s:
            qkv_x_got = x_send({s: qkv_y[s]}) if s == last else {**qkv_x_got, **x_send({s: qkv_y[s]})}
    out_x = x_add([out_y[:, :, :own]], out_x_got)
    qkv_x = x_add(qkv_y, [step(v) for v in qkv_x_got.values()])
    a_x = jnp.concatenate([qkv_x, out_x], axis=2)
    for bit in far_bits:
        n = a_x.shape[0] // 2
        mine_bit = (d >> bit) & 1
        sent = lax.dynamic_slice_in_dim(a_x, (1 - mine_bit) * n, n, 0)
        kept = lax.dynamic_slice_in_dim(a_x, mine_bit * n, n, 0)
        a_x = kept.astype(F32) + over_dp(sent, bit).astype(F32)
        if n > 1:
            a_x = a_x.astype(BF)
    sum_a = a_x[0].astype(F32)
    sum_qkv, sum_out = sum_a[:, : 3 * own].reshape(blk, 3, own), sum_a[:, 3 * own :]

    grad_mod = jnp.stack(
        [
            grad_shift_one,
            grad_scale_one,
            grad_gate_one,
            grad_shift_two,
            grad_scale_two,
            grad_gate_two,
        ],
        axis=1,
    ).astype(BF)
    grad_mod = grad_mod.reshape(mine * 6, full)
    grad_mod = regroup(
        [
            over_mp(dot(grad_mod, p, NT, BF).reshape(mine, 6 * own), s)
            for s, p in enumerate(spreads)
        ]
    )
    grad_mod_all = grad_mod
    for bit in bits:
        grad_mod_all = jnp.concatenate([grad_mod_all, over_dp(grad_mod_all, bit)], 0)
    sum_ada = dot(silu_low, grad_mod_all, TN).reshape(blk, 6, own)
    grad_b_ada = jnp.sum(grad_mod_all.astype(F32), axis=0).reshape(6, own)
    grad_silu = dot(grad_mod_all, w_ada_flat, NT).reshape(nd, lat_dev * blk)
    grad_silu = exact_dot(place_hot.astype(F32), grad_silu, TN).reshape(nd, lat_dev, blk)
    grad_silu = lax.all_to_all(grad_silu, "dp", 0, 0)
    grad_silu = jnp.swapaxes(grad_silu, 0, 1).reshape(lat_dev, nm, own)
    grad_silu = sum(
        over_mp(lax.dynamic_index_in_dim(grad_silu, m ^ s, 1, keepdims=False), s) for s in shifts
    )
    cond_grad = jax.vjp(jax.nn.silu, condition.astype(F32))[1](grad_silu)[0]

    wide = jnp.stack([column_sums(grad_attended), column_sums(grad_branch)])
    bias_own = 0.0
    for s in shifts:
        narrow = exact_dot(wide, spreads[s].astype(F32), NT)
        piece = jnp.concatenate(
            [
                column_sums(grad_qkvs[s][:, :own]),
                column_sums(grad_qkvs[s][:, 2 * own :]),
                column_sums(grad_hiddens[s]),
                narrow.reshape(-1),
            ]
        )
        bias_own = bias_own + over_mp(piece, s)
    for bit in bits:
        bias_own = bias_own + over_dp(bias_own, bit)
    out_b_qv = bias_own[: 2 * own].reshape(2, own)
    out_b_one = bias_own[2 * own : 2 * own + ff]
    out_b_out = bias_own[2 * own + ff : 3 * own + ff]
    out_b_two = bias_own[3 * own + ff :]

    def put(got):
        return lax.dot_general(
            regroup(got), hot, (((1,), (1,)), ((0,), (0,))), preferred_element_type=F32
        )

    taken = jnp.sum(hot.astype(F32), axis=1)[:, None, :] > 0.5
    output = jnp.where(taken, put(fresh_got), inputs.astype(F32)).astype(BF)
    input_grad = jnp.where(
        taken, put(grad_got), cotangent.astype(F32) * row_scale[:, None, None]
    )
    return (
        output,
        input_grad,
        cond_grad,
        sum_qkv,
        out_b_qv,
        sum_out.T,
        out_b_out,
        sum_one,
        out_b_one,
        sum_two.T,
        out_b_two,
        sum_ada,
        grad_b_ada,
    )


def solution(mesh):
    placed = (
        P("dp", "mp", None),
        P("dp", "mp"),
        P("dp", "mp", None),
        P("dp", None),
        P("dp"),
        P("dp"),
        P("dp", None, "mp"),
        P(None, "mp"),
        P("mp", "dp"),
        P("mp"),
        P("dp", "mp"),
        P("mp"),
        P("mp", "dp"),
        P("mp"),
        P("dp", None, "mp"),
        P(None, "mp"),
    )
    return jax.shard_map(
        local,
        mesh=mesh,
        in_specs=placed,
        out_specs=(
            P("dp", "mp", None),
            P("dp", "mp", None),
            P("dp", "mp"),
            P("dp", None, "mp"),
            P(None, "mp"),
            P("mp", "dp"),
            P("mp"),
            P("dp", "mp"),
            P("mp"),
            P("mp", "dp"),
            P("mp"),
            P("dp", None, "mp"),
            P(None, "mp"),
        ),
        check_vma=False,
    )
```

```python
from functools import partial
import math

import jax
import jax.numpy as jnp
from jax import lax
from jax.experimental import pallas as pl
from jax.experimental.pallas import tpu as pltpu
from jax.sharding import PartitionSpec as P

HD = 72
EPS = 1e-06
BF = jnp.bfloat16
F32 = jnp.float32
NN = ((1,), (0,))
NT = ((1,), (1,))
TN = ((0,), (0,))


def dot(left, right, dims, kind=F32):
    return lax.dot_general(left, right, (dims, ((), ())), preferred_element_type=kind)


def exact_dot(left, right, dims):
    return lax.dot_general(
        left,
        right,
        (dims, ((), ())),
        precision=lax.Precision.HIGHEST,
        preferred_element_type=F32,
    )


class Steps:
    def __init__(self):
        self.seen = ()

    def __call__(self, *values):
        out = lax.optimization_barrier((*values, *self.seen))[: len(values)]
        self.seen = out
        return out[0] if len(values) == 1 else out


def attend_kernel(heads, counts, qkv_ref, out_ref):
    count = counts[pl.program_id(0)]
    keep, own = out_ref.shape
    inv_root = 1.0 / math.sqrt(HD)
    valid = lax.broadcasted_iota(jnp.int32, (keep, keep), 1) < count
    for h in range(heads):
        a = HD * h
        q, k = qkv_ref[:, a : a + HD], qkv_ref[:, own + a : own + a + HD]
        v = qkv_ref[:, 2 * own + a : 2 * own + a + HD]
        scores = jnp.where(valid, dot(q, k, NT) * inv_root, -1e30)
        power = jnp.exp(scores - jnp.max(scores, axis=1, keepdims=True))
        probability = power / jnp.sum(power, axis=1, keepdims=True)
        out_ref[:, a : a + HD] = dot(probability.astype(BF), v, NN).astype(BF)


def attend_back_kernel(heads, counts, qkv_ref, g_ref, out_ref):
    count = counts[pl.program_id(0)]
    keep, own = g_ref.shape
    inv_root = 1.0 / math.sqrt(HD)
    valid = lax.broadcasted_iota(jnp.int32, (keep, keep), 0) < count
    for h in range(heads):
        a = HD * h
        q, k = qkv_ref[:, a : a + HD], qkv_ref[:, own + a : own + a + HD]
        v, g = qkv_ref[:, 2 * own + a : 2 * own + a + HD], g_ref[:, a : a + HD]
        scores = jnp.where(valid, dot(k, q, NT) * inv_root, -1e30)
        power = jnp.exp(scores - jnp.max(scores, axis=0, keepdims=True))
        probability = power / jnp.sum(power, axis=0, keepdims=True)
        grad_prob = dot(v, g, NT)
        delta = jnp.sum(grad_prob * probability, axis=0, keepdims=True)
        grad_scores = (probability * (grad_prob - delta)).astype(BF)
        out_ref[:, a : a + HD] = (dot(grad_scores, k, TN) * inv_root).astype(BF)
        out_ref[:, own + a : own + a + HD] = (dot(grad_scores, q, NN) * inv_root).astype(BF)
        out_ref[:, 2 * own + a : 2 * own + a + HD] = dot(probability.astype(BF), g, NN).astype(
            BF
        )


def attend(counts, qkv, own, keep):
    rows = qkv.shape[0]

    def block(n):
        return pl.BlockSpec((keep, n), lambda i, c: (i, 0))

    return pl.pallas_call(
        partial(attend_kernel, own // HD),
        out_shape=jax.ShapeDtypeStruct((rows, own), BF),
        grid_spec=pltpu.PrefetchScalarGridSpec(
            num_scalar_prefetch=1,
            grid=(rows // keep,),
            in_specs=[block(qkv.shape[1])],
            out_specs=block(own),
        ),
        compiler_params=pltpu.CompilerParams(vmem_limit_bytes=40 * 2**20),
    )(counts, qkv)


def attend_back(counts, qkv, g, keep):
    rows, own = g.shape

    def block(n):
        return pl.BlockSpec((keep, n), lambda i, c: (i, 0))

    return pl.pallas_call(
        partial(attend_back_kernel, own // HD),
        out_shape=jax.ShapeDtypeStruct((rows, 3 * own), BF),
        grid_spec=pltpu.PrefetchScalarGridSpec(
            num_scalar_prefetch=1,
            grid=(rows // keep,),
            in_specs=[block(qkv.shape[1]), block(own)],
            out_specs=block(3 * own),
        ),
        compiler_params=pltpu.CompilerParams(vmem_limit_bytes=40 * 2**20),
    )(counts, qkv, g)


def local(
    inputs,
    condition,
    cotangent,
    kept_rows,
    kept_counts,
    group_tokens,
    w_qkv,
    b_qv,
    w_out,
    b_out,
    w_one,
    b_one,
    w_two,
    b_two,
    w_ada,
    b_ada,
):
    nd, nm = lax.axis_size("dp"), lax.axis_size("mp")
    d, m = lax.axis_index("dp"), lax.axis_index("mp")
    lat_dev, own, seq = inputs.shape
    keep = kept_rows.shape[1]
    full = own * nm
    blk, nb = full // nd, nd // nm
    mine = lat_dev // nm
    rows = mine * keep
    ff = w_one.shape[1]
    half = full // 2
    far_bits = [b for b in reversed(range(2, nd.bit_length() - 1))]
    bits = far_bits + [1, 0]
    zb = 2 ** len(far_bits)
    shifts = range(nm)

    step = Steps()

    def over_dp(v, bit):
        return lax.ppermute(step(v), "dp", [(i, i ^ (1 << bit)) for i in range(nd)])

    def over_mp(v, s):
        if s == 0:
            return v
        return lax.ppermute(step(v), "mp", [(i, i ^ s) for i in range(nm)])

    def rel(place):
        out = jnp.zeros_like(place)
        for k, bit in enumerate(bits):
            out = out | (((place >> k) & 1) << bit)
        return out

    def block_of(place):
        near = place // zb
        return ((place % zb) << 2) | ((d & 3) ^ (((near & 1) << 1) | (near >> 1)))

    def spread(s, kind):
        place = lax.broadcasted_iota(jnp.int32, (own, full), 1)
        feature = lax.broadcasted_iota(jnp.int32, (own, full), 0)
        source = block_of(place // blk)
        wanted = (m ^ s) * nb + feature // blk
        return ((source == wanted) & (place % blk == feature % blk)).astype(kind)

    spreads = [spread(s, BF) for s in shifts]
    place_hot = (
        (d ^ rel(lax.broadcasted_iota(jnp.int32, (nd, nd), 0)))
        == lax.broadcasted_iota(jnp.int32, (nd, nd), 1)
    )
    far_groups = [[low + 4 * k for k in range(zb)] for low in range(4)]

    def group_of(v, s):
        return lax.dynamic_slice_in_dim(v, (m ^ s) * mine, mine, 0)

    def regroup(parts):
        stacked = jnp.stack(parts)
        return jnp.concatenate(
            [lax.dynamic_index_in_dim(stacked, m ^ g, 0, keepdims=False) for g in shifts]
        )

    def send_rows(v):
        return [over_mp(group_of(v, s), s).reshape(rows, own) for s in shifts]

    def to_rows(got):
        return sum(dot(g, p, NN) for g, p in zip(got, spreads))

    def from_rows(v):
        parts = [dot(v, p, NT, BF).reshape(mine, keep, own) for p in spreads]
        return [over_mp(part, s) for s, part in enumerate(parts)]

    def far_gather(v):
        return lax.all_gather(v, "dp", axis=0, tiled=True, axis_index_groups=far_groups)

    def later(vs):
        return [vs[0], *[step(v) for v in vs[1:]]]

    bias_vec = jnp.concatenate([b_qv.reshape(-1), b_one, b_out, b_two])
    bias_size = bias_vec.shape[0]
    bias_rows = -(-bias_size // own)
    bias_vec = jnp.pad(bias_vec, (0, bias_rows * own - bias_size)).reshape(bias_rows, own)
    small = jnp.concatenate([condition, bias_vec], axis=0)
    smalls = [over_mp(small, s) for s in shifts]
    w_a = jnp.concatenate([w_qkv.reshape(blk, 3 * own), w_out.T], axis=1)
    a_z = far_gather(w_a)
    one_z = far_gather(w_one)
    digits = jnp.stack([(group_tokens >> (8 * k)) & 255 for k in range(4)], axis=1)
    pad = -(blk + 4) % 8
    valid = jnp.arange(keep)[None, :] < kept_counts[:, None]
    hot = (
        (kept_rows[:, :, None] == jnp.arange(seq)[None, None, :]) & valid[:, :, None]
    ).astype(BF)

    def pick(source):
        return lax.dot_general(
            hot, source, (((2,), (2,)), ((0,), (0,))), preferred_element_type=BF
        )

    w_a, small = step(w_a, small)
    picked = step(pick(step(inputs)))
    kept_got = send_rows(picked)
    smalls = later(smalls)
    cond_halves = jnp.stack([v[:lat_dev] for v in smalls])
    bias_all = [v[lat_dev:].reshape(-1) for v in smalls]
    cond_full = jnp.concatenate(
        [lax.dynamic_index_in_dim(cond_halves, m ^ g, 0, keepdims=False) for g in shifts], axis=1
    )
    cond_send = step(
        jnp.concatenate(
            [
                jnp.swapaxes(cond_full.reshape(lat_dev, nd, blk), 0, 1),
                jnp.broadcast_to(digits.astype(BF)[None], (nd, lat_dev, 4)),
                jnp.zeros((nd, lat_dev, pad), BF),
            ],
            axis=2,
        )
    )
    cond_got = lax.all_to_all(cond_send, "dp", 0, 0)
    w_two_t = w_two.T
    w_ada_flat = w_ada.reshape(blk, 6 * own)
    two_z = far_gather(w_two_t)
    w_two_t, w_ada_flat, cond_got = step(w_two_t, w_ada_flat, cond_got)
    cond_got = dot(place_hot.astype(BF), cond_got.reshape(nd, -1), NN).reshape(
        nd, lat_dev, blk + 4 + pad
    )
    token_total = sum(
        jnp.sum(cond_got[:, :, blk + k]) * float(256**k) for k in range(4)
    )
    silu_low = jax.nn.silu(cond_got[:, :, :blk].reshape(nd * lat_dev, blk)).astype(BF)
    part = dot(silu_low, w_ada_flat, NN).reshape(nd, lat_dev, 6 * own)
    part = step(part)

    def part_send(part, bit):
        return over_dp(part[part.shape[0] // 2 :], bit)

    def part_add(part, got):
        return part[: part.shape[0] // 2] + got

    def far_mask(place):
        return sum(((place >> k) & 1) << bit for k, bit in enumerate(far_bits))

    def over_far(v, place):
        return lax.ppermute(step(v), "dp", [(i, i ^ far_mask(place)) for i in range(nd)])

    got = part_send(part, 0)
    part = part_add(part, step(got))
    got = part_send(part, 1)

    def core_pair(v):
        return (v, over_dp(v, 0))

    def join(first, second):
        return jnp.stack([first[0], second[0], first[1], second[1]]).reshape(full, -1)

    a_z = step(a_z)
    a_xs = [over_mp(a_z, s) for s in shifts]
    a_y = over_dp(a_z, 1)
    kept_got = later(kept_got)
    kept_slot = step(to_rows(kept_got)).reshape(mine, keep, full)
    part = step(part_add(part, step(got)))
    part_gots = [over_far(part[p], p) for p in range(1, zb)]
    a_zc = core_pair(a_z)
    modulation = part[0] + b_ada.astype(F32).reshape(6 * own)
    for v in part_gots:
        modulation = modulation + step(v)
    modulation = step(modulation)

    def mod_group(s):
        own_part = group_of(modulation, s)
        return jnp.stack([own_part[:, k * own : (k + 1) * own] for k in range(6)]).reshape(
            6 * mine, own
        )

    mod_got = [over_mp(mod_group(s), s) for s in shifts]
    cot_picked = step(pick(step(cotangent)))
    cot_parts = step(*[group_of(cot_picked, s).reshape(rows, own) for s in shifts])
    cot_parts = cot_parts if nm > 1 else [cot_parts]
    mod_got = later(mod_got)
    a_xs = later(a_xs)
    a_y = step(a_y)
    a_xys = [over_mp(a_y, s) for s in shifts]
    one_z = step(one_z)
    one_y = over_dp(one_z, 1)
    a_yc = core_pair(a_y)
    mod_rows = sum(
        exact_dot(v, p.astype(F32), NN) for v, p in zip(mod_got, spreads)
    ).reshape(6, mine, full)
    shift_one, scale_one, gate_one, shift_two, scale_two, gate_two = [
        mod_rows[k, :, None, :] for k in range(6)
    ]
    bias_qv = [v[: 2 * own].reshape(2, own).astype(F32) for v in bias_all]
    bias_one = [v[2 * own : 2 * own + ff].astype(F32) for v in bias_all]
    bias_wide = sum(
        dot(v[2 * own + ff : bias_size].reshape(2, own), p, NN) for v, p in zip(bias_all, spreads)
    )
    row_scale = lat_dev * nd * group_tokens.astype(F32) / token_total
    own_scale = group_of(row_scale, 0)[:, None, None]
    own_counts = group_of(kept_counts, 0)

    def cubes(v):
        return v.reshape(mine, keep, -1)

    def flat(v):
        return v.reshape(rows, -1)

    def column_sums(v):
        return dot(jnp.ones((8, rows), BF), v, NN)[0]

    def normalize(v):
        center = jnp.mean(v, axis=-1, keepdims=True)
        var = jnp.mean(v * v, axis=-1, keepdims=True) - center * center
        scaled = lax.rsqrt(var + EPS)
        return (v - center) * scaled, scaled

    def norm_back(g, normed, scaled):
        a = jnp.mean(g, axis=-1, keepdims=True)
        b = jnp.mean(g * normed, axis=-1, keepdims=True)
        return (g - a - normed * b) * scaled

    normed_one, scaled_one = normalize(kept_slot)
    first_low = flat((normed_one * (1.0 + scale_one) + shift_one).astype(BF))
    first_low = step(first_low)
    w_as, qkvs, mixtures, wo_t = [], [], [], []
    attended = bias_wide[0]
    a_pairs = {0: (a_zc, a_yc)}
    for s in shifts:
        first, second = a_pairs[s]
        w_as.append(join((first[0], step(first[1])), (second[0], step(second[1]))))
        bias = jnp.concatenate(
            [bias_qv[s][0], jnp.zeros((own,), F32), bias_qv[s][1], jnp.zeros((own,), F32)]
        )
        qkv = step((dot(first_low, w_as[s], NN) + bias).astype(BF))
        qkvs.append(qkv)
        mixture = step(attend(own_counts, qkv, own, keep))
        mixtures.append(mixture)
        if s == 0:
            a_xys = later(a_xys)
            one_y = step(one_y)
            one_xs = [over_mp(one_z, t) for t in shifts]
            two_z = step(two_z)
            two_y = over_dp(two_z, 1)
            for t in shifts[1:]:
                a_pairs[t] = (core_pair(a_xs[t]), core_pair(a_xys[t]))
        wo_t.append(w_as[s][:, 3 * own :])
        attended = step(attended + dot(mixture, wo_t[s], NT))
    one_zc, one_yc = core_pair(one_z), core_pair(one_y)
    one_xs = later(one_xs)
    two_y = step(two_y)
    two_xs = [over_mp(two_z, s) for s in shifts]
    one_xys = [one_y, *[over_dp(v, 1) for v in one_xs[1:]]]
    g_one = {0: (one_zc, one_yc)}
    attended = cubes(attended)
    residual = kept_slot + gate_one * attended
    normed_two, scaled_two = normalize(residual)
    second_low = flat((normed_two * (1.0 + scale_two) + shift_two).astype(BF))
    second_low = step(second_low)
    g_two = {0: (core_pair(two_z), core_pair(two_y))}
    branch = bias_wide[1]
    w1, w2t, acts, slopes = [], [], [], []
    root = math.sqrt(2.0 / math.pi)
    for s in shifts:
        first, second = g_one[s]
        w1.append(join((first[0], step(first[1])), (second[0], step(second[1]))))
        hidden = dot(second_low, w1[s], NN) + bias_one[s]
        square = hidden * hidden
        bend = jnp.tanh(root * hidden * (1.0 + 0.044715 * square))
        act = (0.5 * hidden * (1.0 + bend)).astype(BF)
        slope = 0.5 * (1.0 + bend) + 0.5 * root * hidden * (1.0 - bend * bend) * (
            1.0 + 3.0 * 0.044715 * square
        )
        act, slope = step(act, slope)
        acts.append(act)
        slopes.append(slope)
        if s == 0:
            two_xs = later(two_xs)
            one_xys = later(one_xys)
            cols = ff // 384 * 128
            two_xys = [None]
            for t in shifts[1:]:
                two_xys.append(
                    (over_mp(two_y[:, :cols], t), over_dp(two_xs[t][:, cols:], 1))
                )
            for t in shifts[1:]:
                g_one[t] = (core_pair(one_xs[t]), core_pair(one_xys[t]))
            mixture_all = jnp.concatenate(mixtures, axis=1)
            cot_got = [over_mp(v, t) for t, v in enumerate(cot_parts)]
        if s == 1:
            for t in shifts[1:]:
                ends = [core_pair(step(v)) for v in two_xys[t]]
                g_two[t] = (core_pair(two_xs[t]), ends)
            cot_got = later(cot_got)
        first, second = g_two[s]
        if s:
            second = [(v[0], step(v[1])) for v in second]
            second = [jnp.concatenate([v[k] for v in second], axis=1) for k in range(2)]
        else:
            second = (second[0], step(second[1]))
        w2t.append(join((first[0], step(first[1])), second))
        branch = step(branch + dot(act, w2t[s], NT))
    branch = cubes(branch)
    result = residual + gate_two * branch
    result_low = flat(result).astype(BF)

    def add(a, b):
        return (a.astype(F32) + b.astype(F32)).astype(BF)

    near = zb * blk

    def keep_sum(low_side, v, got):
        return (dot(low_side, v, TN) + got.astype(F32)).astype(BF)

    def y_send(v):
        return over_dp(v[near:], 1)

    def y_add(v, got):
        return add(v[:near], got)

    def x_send(vs):
        return {s: over_mp(v, s) for s, v in vs.items() if s}

    def x_add(vs, got):
        total = vs[0].astype(F32)
        for v in got:
            total = total + v.astype(F32)
        return total.astype(BF)

    cot_rows = to_rows(cot_got).reshape(mine, keep, full)
    grad_result = cot_rows * own_scale
    grad_branch = flat((gate_two * grad_result).astype(BF))
    order = list(reversed(shifts))

    def far_scatter(v):
        v = v.reshape(zb * blk, -1)
        v = lax.psum_scatter(
            v, "dp", scatter_dimension=0, tiled=True, axis_index_groups=far_groups
        )
        return v

    low, high, grad_branch = step(grad_branch[:, :half], grad_branch[:, half:], grad_branch)
    two_got, two_kept, two_y_got, two_y, two_x_got = {}, {}, {}, {}, {}
    grad_hiddens = [None] * nm
    last = order[0]
    for s in order:
        two_got[s] = over_dp(step(dot(high, acts[s], TN, BF)), 0)
    for s in order:
        grad_hiddens[s] = step((dot(step(grad_branch), w2t[s], NN) * slopes[s]).astype(BF))
        two_kept[s] = step(keep_sum(low, acts[s], step(two_got[s])))
        two_y_got[s] = y_send(two_kept[s])
    low, high = step(second_low[:, :half], second_low[:, half:])
    one_got, one_kept, one_x_got = {}, {}, {}
    for s in order:
        one_got[s] = over_dp(step(dot(high, grad_hiddens[s], TN, BF)), 0)
    for s in order:
        one_kept[s] = step(keep_sum(low, grad_hiddens[s], step(one_got[s])))
        if s:
            one_x_got[s] = (over_mp(one_kept[s][near:], s), over_mp(one_kept[s][:near], s))
    grad_second = None
    for s in shifts:
        piece = dot(step(grad_hiddens[s]), w1[s], NT)
        grad_second = step(piece if grad_second is None else grad_second + piece)
    for s in order[:-1]:
        two_y[s] = step(y_add(two_kept[s], step(two_y_got[s])))
        two_x_got[s] = over_mp(two_y[s], s)
    grad_second = cubes(step(grad_second))
    grad_shift_two = jnp.sum(grad_second, axis=1)
    grad_scale_two = jnp.sum(grad_second * normed_two, axis=1)
    grad_residual = grad_result + norm_back(
        grad_second * (1.0 + scale_two), normed_two, scaled_two
    )
    grad_attended = flat((gate_one * grad_residual).astype(BF))
    low, high, grad_attended = step(
        grad_attended[:, :half], grad_attended[:, half:], grad_attended
    )
    out_got = over_dp(step(dot(high, mixture_all, TN, BF)), 0)
    grad_mixtures = [step(dot(step(grad_attended), w, NN, BF)) for w in wo_t]
    two_y[0] = step(y_add(two_kept[0], step(two_y_got[0])))
    one_high = step(x_add([one_kept[0][near:]], [step(v[0]) for v in one_x_got.values()]))
    one_y_got = over_dp(one_high, 1)
    out_kept = step(keep_sum(low, mixture_all, step(out_got)))
    out_y_got = y_send(out_kept)
    grad_qkvs, qkv_got, qk_kept, v_kept, qk_y_got, qk_y = [None] * nm, {}, {}, {}, {}, {}
    first_half, second_half = step(first_low[:, :half], first_low[:, half:])
    for s in order:
        grad_qkvs[s] = step(attend_back(step(own_counts), qkvs[s], grad_mixtures[s], keep))
        if s == last:
            one_x_got = {t: step(v[1]) for t, v in one_x_got.items()}
            one_low = step(x_add([one_kept[0][:near]], one_x_got.values()))
        else:
            one_y_got = step(one_y_got) if s == 0 else one_y_got
        qkv_got[s] = over_dp(step(dot(second_half, grad_qkvs[s], TN, BF)), 0)
    two_x = step(x_add(two_y, [step(v) for v in two_x_got.values()]))
    sum_two = far_scatter(two_x)
    one_y = step(add(one_low, one_y_got))
    fresh_got = from_rows(result_low)
    sum_one = far_scatter(one_y)
    v_x_got = {}
    for s in order:
        kept = step(keep_sum(first_half, grad_qkvs[s], step(qkv_got[s])))
        qk_kept[s], v_kept[s] = kept[:, : 2 * own], kept[:, 2 * own :]
        qk_y_got[s] = y_send(qk_kept[s])
        if s:
            v_x_got[s] = over_mp(v_kept[s], s)
    out_y = step(y_add(out_kept, step(out_y_got)))
    out_x_got = [over_mp(out_y[:, s * own : (s + 1) * own], s) for s in shifts[1:]]
    w_qkvs = [w[:, : 3 * own] for w in w_as]
    grad_first = step(dot(step(grad_qkvs[0]), w_qkvs[0], NT))
    fresh_got = later(fresh_got)
    qk_y[last] = step(y_add(qk_kept[last], step(qk_y_got[last])))
    qk_x_got = {last: over_mp(qk_y[last], last)} if last else {}
    for s in shifts[1:]:
        grad_first = step(grad_first + dot(step(grad_qkvs[s]), w_qkvs[s], NT))
    v_x = step(x_add(v_kept, [step(v) for v in v_x_got.values()]))
    v_y_got = y_send(v_x)
    grad_first = cubes(step(grad_first))
    grad_shift_one = jnp.sum(grad_first, axis=1)
    grad_scale_one = jnp.sum(grad_first * normed_one, axis=1)
    grad_gate_two = jnp.sum(grad_result * branch, axis=1)
    grad_gate_one = jnp.sum(grad_residual * attended, axis=1)
    grad_mod = jnp.stack(
        [
            grad_shift_one,
            grad_scale_one,
            grad_gate_one,
            grad_shift_two,
            grad_scale_two,
            grad_gate_two,
        ],
        axis=1,
    ).astype(BF)
    grad_mod = step(grad_mod.reshape(mine * 6, full))
    if last:
        qk_x_got[last] = step(qk_x_got[last])
    out_x_got = [step(v) for v in out_x_got]
    mod_back = [
        over_mp(dot(grad_mod, p, NT, BF).reshape(mine, 6 * own), s)
        for s, p in enumerate(spreads)
    ]
    for s in order[1:]:
        qk_y[s] = step(y_add(qk_kept[s], step(qk_y_got[s])))
        if s:
            qk_x_got[s] = over_mp(qk_y[s], s)
    mod_back = step(regroup(later(mod_back)))
    mod_gots = [over_far(mod_back, p) for p in range(1, zb)]
    out_x = x_add([out_y[:, :own]], out_x_got)
    qk_x = step(x_add(qk_y, [step(v) for v in qk_x_got.values()]))
    v_y = y_add(v_x, step(v_y_got))
    a_x = step(jnp.concatenate([qk_x, v_y, out_x], axis=1)).reshape(zb, blk, 4 * own)
    far_at = d >> 2
    far_kept = lax.dynamic_index_in_dim(a_x, far_at, 0, keepdims=False)
    far_sent = [
        lax.dynamic_index_in_dim(a_x, far_at ^ k, 0, keepdims=False) for k in range(1, zb)
    ]
    mod_gots = [step(v) for v in mod_gots]
    grad_mod_all = step(jnp.concatenate([mod_back, *mod_gots], 0))
    mod_got = over_dp(grad_mod_all, 1)
    far_got = [
        lax.ppermute(step(v), "dp", [(i, i ^ ((k + 1) << 2)) for i in range(nd)])
        for k, v in enumerate(far_sent)
    ]
    grad_kept = grad_residual + norm_back(
        step(grad_first) * (1.0 + scale_one), normed_one, scaled_one
    )
    grad_low = step(flat(grad_kept).astype(BF))
    grad_mod_all = step(jnp.concatenate([grad_mod_all, step(mod_got)], 0))
    mod_got = over_dp(grad_mod_all, 0)
    grad_got = from_rows(grad_low)
    grad_mod_all = step(jnp.concatenate([grad_mod_all, step(mod_got)], 0))
    grad_silu = dot(grad_mod_all, w_ada_flat, NT).reshape(nd, lat_dev * blk)
    grad_silu = exact_dot(place_hot.astype(F32), grad_silu, TN).reshape(nd, lat_dev, blk)
    grad_silu = lax.all_to_all(step(grad_silu), "dp", 0, 0)
    grad_attended, grad_branch, *held = step(
        grad_attended, grad_branch, *grad_qkvs, *grad_hiddens
    )
    grad_qkvs, grad_hiddens = held[:nm], held[nm:]
    bias_wide_sums = step(jnp.stack([column_sums(grad_attended), column_sums(grad_branch)]))
    grad_silu = step(grad_silu)
    grad_silu = jnp.swapaxes(grad_silu, 0, 1).reshape(lat_dev, nm, own)
    silu_got = [
        over_mp(lax.dynamic_index_in_dim(grad_silu, m ^ s, 1, keepdims=False), s) for s in shifts
    ]
    bias_own = 0.0
    for s in shifts:
        narrow = exact_dot(bias_wide_sums, spreads[s].astype(F32), NT)
        piece = jnp.concatenate(
            [
                column_sums(grad_qkvs[s][:, :own]),
                column_sums(grad_qkvs[s][:, 2 * own :]),
                column_sums(grad_hiddens[s]),
                narrow.reshape(-1),
            ]
        )
        bias_own = bias_own + step(over_mp(piece, s))
    bias_gots = [over_far(bias_own, p) for p in range(1, zb)]
    taken = jnp.sum(hot.astype(F32), axis=1)[:, None, :] > 0.5

    def put(got):
        return lax.dot_general(
            regroup(got), hot, (((1,), (1,)), ((0,), (0,))), preferred_element_type=F32
        )

    sum_ada = dot(silu_low, grad_mod_all, TN).reshape(blk, 6, own)
    grad_b_ada = jnp.sum(grad_mod_all.astype(F32), axis=0).reshape(6, own)
    sum_ada, grad_b_ada = step(sum_ada, grad_b_ada)
    for v in bias_gots:
        bias_own = bias_own + step(v)
    bias_got = over_dp(bias_own, 1)
    output = jnp.where(taken, put(fresh_got), inputs.astype(F32)).astype(BF)
    output = step(output)
    bias_own = step(bias_own + bias_got)
    bias_got = over_dp(bias_own, 0)
    sum_two, sum_one = step(sum_two, sum_one)
    sum_two, sum_one = sum_two.astype(F32), sum_one.astype(F32)
    total = far_kept.astype(F32)
    for v in far_got:
        total = total + v.astype(F32)
    total = step(total)
    input_grad = jnp.where(
        taken, put(later(grad_got)), cotangent.astype(F32) * row_scale[:, None, None]
    )
    input_grad = step(input_grad)
    bias_own = bias_own + bias_got
    cond_grad = jax.vjp(jax.nn.silu, condition.astype(F32))[1](sum(silu_got))[0]
    sum_qkv, sum_out = total[:, : 3 * own].reshape(blk, 3, own), total[:, 3 * own :]

    out_b_qv = bias_own[: 2 * own].reshape(2, own)
    out_b_one = bias_own[2 * own : 2 * own + ff]
    out_b_out = bias_own[2 * own + ff : 3 * own + ff]
    out_b_two = bias_own[3 * own + ff :]

    return (
        output,
        input_grad,
        cond_grad,
        sum_qkv,
        out_b_qv,
        sum_out.T,
        out_b_out,
        sum_one,
        out_b_one,
        sum_two.T,
        out_b_two,
        sum_ada,
        grad_b_ada,
    )


def solution(mesh):
    placed = (
        P("dp", "mp", None),
        P("dp", "mp"),
        P("dp", "mp", None),
        P("dp", None),
        P("dp"),
        P("dp"),
        P("dp", None, "mp"),
        P(None, "mp"),
        P("mp", "dp"),
        P("mp"),
        P("dp", "mp"),
        P("mp"),
        P("mp", "dp"),
        P("mp"),
        P("dp", None, "mp"),
        P(None, "mp"),
    )
    return jax.shard_map(
        local,
        mesh=mesh,
        in_specs=placed,
        out_specs=(
            P("dp", "mp", None),
            P("dp", "mp", None),
            P("dp", "mp"),
            P("dp", None, "mp"),
            P(None, "mp"),
            P("mp", "dp"),
            P("mp"),
            P("dp", "mp"),
            P("mp"),
            P("mp", "dp"),
            P("mp"),
            P("dp", None, "mp"),
            P(None, "mp"),
        ),
        check_vma=False,
    )
```

```python
from functools import partial
import math

import jax
import jax.numpy as jnp
from jax import lax
from jax.experimental import pallas as pl
from jax.experimental.pallas import tpu as pltpu
from jax.sharding import PartitionSpec as P

HD = 72
EPS = 1e-06
BF = jnp.bfloat16
F32 = jnp.float32
NN = ((1,), (0,))
NT = ((1,), (1,))
TN = ((0,), (0,))


def dot(left, right, dims, kind=F32):
    return lax.dot_general(left, right, (dims, ((), ())), preferred_element_type=kind)


def exact_dot(left, right, dims):
    return lax.dot_general(
        left,
        right,
        (dims, ((), ())),
        precision=lax.Precision.HIGHEST,
        preferred_element_type=F32,
    )


class Steps:
    def __init__(self):
        self.seen = ()

    def __call__(self, *values):
        out = lax.optimization_barrier((*values, *self.seen))[: len(values)]
        self.seen = out
        return out[0] if len(values) == 1 else out


def attend_kernel(heads, counts, qkv_ref, out_ref):
    count = counts[pl.program_id(0)]
    keep, own = out_ref.shape
    inv_root = 1.0 / math.sqrt(HD)
    valid = lax.broadcasted_iota(jnp.int32, (keep, keep), 1) < count
    for h in range(heads):
        a = HD * h
        q, k = qkv_ref[:, a : a + HD], qkv_ref[:, own + a : own + a + HD]
        v = qkv_ref[:, 2 * own + a : 2 * own + a + HD]
        scores = jnp.where(valid, dot(q, k, NT) * inv_root, -1e30)
        power = jnp.exp(scores - jnp.max(scores, axis=1, keepdims=True))
        probability = power / jnp.sum(power, axis=1, keepdims=True)
        out_ref[:, a : a + HD] = dot(probability.astype(BF), v, NN).astype(BF)


def attend_back_kernel(heads, counts, qkv_ref, g_ref, out_ref):
    count = counts[pl.program_id(0)]
    keep, own = g_ref.shape
    inv_root = 1.0 / math.sqrt(HD)
    valid = lax.broadcasted_iota(jnp.int32, (keep, keep), 0) < count
    for h in range(heads):
        a = HD * h
        q, k = qkv_ref[:, a : a + HD], qkv_ref[:, own + a : own + a + HD]
        v, g = qkv_ref[:, 2 * own + a : 2 * own + a + HD], g_ref[:, a : a + HD]
        scores = jnp.where(valid, dot(k, q, NT) * inv_root, -1e30)
        power = jnp.exp(scores - jnp.max(scores, axis=0, keepdims=True))
        probability = power / jnp.sum(power, axis=0, keepdims=True)
        grad_prob = dot(v, g, NT)
        delta = jnp.sum(grad_prob * probability, axis=0, keepdims=True)
        grad_scores = (probability * (grad_prob - delta)).astype(BF)
        out_ref[:, a : a + HD] = (dot(grad_scores, k, TN) * inv_root).astype(BF)
        out_ref[:, own + a : own + a + HD] = (dot(grad_scores, q, NN) * inv_root).astype(BF)
        out_ref[:, 2 * own + a : 2 * own + a + HD] = dot(probability.astype(BF), g, NN).astype(
            BF
        )


def attend(counts, qkv, own, keep):
    rows = qkv.shape[0]

    def block(n):
        return pl.BlockSpec((keep, n), lambda i, c: (i, 0))

    return pl.pallas_call(
        partial(attend_kernel, own // HD),
        out_shape=jax.ShapeDtypeStruct((rows, own), BF),
        grid_spec=pltpu.PrefetchScalarGridSpec(
            num_scalar_prefetch=1,
            grid=(rows // keep,),
            in_specs=[block(qkv.shape[1])],
            out_specs=block(own),
        ),
        compiler_params=pltpu.CompilerParams(vmem_limit_bytes=40 * 2**20),
    )(counts, qkv)


def attend_back(counts, qkv, g, keep):
    rows, own = g.shape

    def block(n):
        return pl.BlockSpec((keep, n), lambda i, c: (i, 0))

    return pl.pallas_call(
        partial(attend_back_kernel, own // HD),
        out_shape=jax.ShapeDtypeStruct((rows, 3 * own), BF),
        grid_spec=pltpu.PrefetchScalarGridSpec(
            num_scalar_prefetch=1,
            grid=(rows // keep,),
            in_specs=[block(qkv.shape[1]), block(own)],
            out_specs=block(3 * own),
        ),
        compiler_params=pltpu.CompilerParams(vmem_limit_bytes=40 * 2**20),
    )(counts, qkv, g)


def local(
    inputs,
    condition,
    cotangent,
    kept_rows,
    kept_counts,
    group_tokens,
    w_qkv,
    b_qv,
    w_out,
    b_out,
    w_one,
    b_one,
    w_two,
    b_two,
    w_ada,
    b_ada,
):
    nd, nm = lax.axis_size("dp"), lax.axis_size("mp")
    d, m = lax.axis_index("dp"), lax.axis_index("mp")
    lat_dev, own, seq = inputs.shape
    keep = kept_rows.shape[1]
    full = own * nm
    blk, nb = full // nd, nd // nm
    mine = lat_dev // nm
    rows = mine * keep
    ff = w_one.shape[1]
    half = full // 2
    far_bits = [b for b in reversed(range(2, nd.bit_length() - 1))]
    bits = far_bits + [1, 0]
    zb = 2 ** len(far_bits)
    shifts = range(nm)

    step = Steps()

    def over_dp(v, bit):
        return lax.ppermute(step(v), "dp", [(i, i ^ (1 << bit)) for i in range(nd)])

    def over_mp(v, s):
        if s == 0:
            return v
        return lax.ppermute(step(v), "mp", [(i, i ^ s) for i in range(nm)])

    def rel(place):
        out = jnp.zeros_like(place)
        for k, bit in enumerate(bits):
            out = out | (((place >> k) & 1) << bit)
        return out

    def block_of(place):
        near = place // zb
        return ((place % zb) << 2) | ((d & 3) ^ (((near & 1) << 1) | (near >> 1)))

    def spread(s, kind):
        place = lax.broadcasted_iota(jnp.int32, (own, full), 1)
        feature = lax.broadcasted_iota(jnp.int32, (own, full), 0)
        source = block_of(place // blk)
        wanted = (m ^ s) * nb + feature // blk
        return ((source == wanted) & (place % blk == feature % blk)).astype(kind)

    spreads = [spread(s, BF) for s in shifts]
    place_hot = (
        (d ^ rel(lax.broadcasted_iota(jnp.int32, (nd, nd), 0)))
        == lax.broadcasted_iota(jnp.int32, (nd, nd), 1)
    )
    far_groups = [[low + 4 * k for k in range(zb)] for low in range(4)]

    def group_of(v, s):
        return lax.dynamic_slice_in_dim(v, (m ^ s) * mine, mine, 0)

    def regroup(parts):
        stacked = jnp.stack(parts)
        return jnp.concatenate(
            [lax.dynamic_index_in_dim(stacked, m ^ g, 0, keepdims=False) for g in shifts]
        )

    def send_rows(v):
        return [over_mp(group_of(v, s), s).reshape(rows, own) for s in shifts]

    def to_rows(got):
        return sum(dot(g, p, NN) for g, p in zip(got, spreads))

    def from_rows(v):
        parts = [dot(v, p, NT, BF).reshape(mine, keep, own) for p in spreads]
        return [over_mp(part, s) for s, part in enumerate(parts)]

    def far_gather(v):
        return lax.all_gather(v, "dp", axis=0, tiled=True, axis_index_groups=far_groups)

    def later(vs):
        return [vs[0], *[step(v) for v in vs[1:]]]

    bias_vec = jnp.concatenate([b_qv.reshape(-1), b_one, b_out, b_two])
    bias_size = bias_vec.shape[0]
    bias_rows = -(-bias_size // own)
    bias_vec = jnp.pad(bias_vec, (0, bias_rows * own - bias_size)).reshape(bias_rows, own)
    small = jnp.concatenate([condition, bias_vec], axis=0)
    smalls = [over_mp(small, s) for s in shifts]
    w_a = jnp.concatenate([w_qkv.reshape(blk, 3 * own), w_out.T], axis=1)
    a_z = far_gather(w_a)
    one_z = far_gather(w_one)
    digits = jnp.stack([(group_tokens >> (8 * k)) & 255 for k in range(4)], axis=1)
    pad = -(blk + 4) % 8
    valid = jnp.arange(keep)[None, :] < kept_counts[:, None]
    hot = (
        (kept_rows[:, :, None] == jnp.arange(seq)[None, None, :]) & valid[:, :, None]
    ).astype(BF)

    def pick(source):
        return lax.dot_general(
            hot, source, (((2,), (2,)), ((0,), (0,))), preferred_element_type=BF
        )

    w_a, small = step(w_a, small)
    picked = step(pick(step(inputs)))
    kept_got = send_rows(picked)
    smalls = later(smalls)
    cond_halves = jnp.stack([v[:lat_dev] for v in smalls])
    bias_all = [v[lat_dev:].reshape(-1) for v in smalls]
    cond_full = jnp.concatenate(
        [lax.dynamic_index_in_dim(cond_halves, m ^ g, 0, keepdims=False) for g in shifts], axis=1
    )
    cond_send = step(
        jnp.concatenate(
            [
                jnp.swapaxes(cond_full.reshape(lat_dev, nd, blk), 0, 1),
                jnp.broadcast_to(digits.astype(BF)[None], (nd, lat_dev, 4)),
                jnp.zeros((nd, lat_dev, pad), BF),
            ],
            axis=2,
        )
    )
    cond_got = lax.all_to_all(cond_send, "dp", 0, 0)
    w_two_t = w_two.T
    w_ada_flat = w_ada.reshape(blk, 6 * own)
    two_z = far_gather(w_two_t)
    w_two_t, w_ada_flat, cond_got = step(w_two_t, w_ada_flat, cond_got)
    cond_got = dot(place_hot.astype(BF), cond_got.reshape(nd, -1), NN).reshape(
        nd, lat_dev, blk + 4 + pad
    )
    token_total = sum(
        jnp.sum(cond_got[:, :, blk + k]) * float(256**k) for k in range(4)
    )
    silu_low = jax.nn.silu(cond_got[:, :, :blk].reshape(nd * lat_dev, blk)).astype(BF)
    part = dot(silu_low, w_ada_flat, NN).reshape(nd, lat_dev, 6 * own)
    part = step(part)

    def part_send(part, bit):
        return over_dp(part[part.shape[0] // 2 :], bit)

    def part_add(part, got):
        return part[: part.shape[0] // 2] + got

    def far_mask(place):
        return sum(((place >> k) & 1) << bit for k, bit in enumerate(far_bits))

    def over_far(v, place):
        return lax.ppermute(step(v), "dp", [(i, i ^ far_mask(place)) for i in range(nd)])

    got = part_send(part, 0)
    part = part_add(part, step(got))
    got = part_send(part, 1)

    def core_pair(v):
        return (v, over_dp(v, 0))

    def join(first, second):
        return jnp.stack([first[0], second[0], first[1], second[1]]).reshape(full, -1)

    a_z = step(a_z)
    a_xs = [over_mp(a_z, s) for s in shifts]
    a_y = over_dp(a_z, 1)
    kept_got = later(kept_got)
    kept_slot = step(to_rows(kept_got)).reshape(mine, keep, full)
    part = step(part_add(part, step(got)))
    part_gots = [over_far(part[p], p) for p in range(1, zb)]
    a_zc = core_pair(a_z)
    cot_picked = step(pick(step(cotangent)))
    cot_parts = step(*[group_of(cot_picked, s).reshape(rows, own) for s in shifts])
    cot_parts = cot_parts if nm > 1 else [cot_parts]
    a_xs = later(a_xs)
    a_y = step(a_y)
    modulation = part[0] + b_ada.astype(F32).reshape(6 * own)
    for v in part_gots:
        modulation = modulation + step(v)
    modulation = step(modulation)

    def mod_group(s):
        own_part = group_of(modulation, s)
        return jnp.stack([own_part[:, k * own : (k + 1) * own] for k in range(6)]).reshape(
            6 * mine, own
        )

    mod_got = [over_mp(mod_group(s), s) for s in shifts]
    a_xys = [over_mp(a_y, s) for s in shifts]
    one_z = step(one_z)
    one_y = over_dp(one_z, 1)
    a_yc = core_pair(a_y)
    mod_got = later(mod_got)
    mod_rows = sum(
        exact_dot(v, p.astype(F32), NN) for v, p in zip(mod_got, spreads)
    ).reshape(6, mine, full)
    shift_one, scale_one, gate_one, shift_two, scale_two, gate_two = [
        mod_rows[k, :, None, :] for k in range(6)
    ]
    bias_qv = [v[: 2 * own].reshape(2, own).astype(F32) for v in bias_all]
    bias_one = [v[2 * own : 2 * own + ff].astype(F32) for v in bias_all]
    bias_wide = sum(
        dot(v[2 * own + ff : bias_size].reshape(2, own), p, NN) for v, p in zip(bias_all, spreads)
    )
    row_scale = lat_dev * nd * group_tokens.astype(F32) / token_total
    own_scale = group_of(row_scale, 0)[:, None, None]
    own_counts = group_of(kept_counts, 0)

    def cubes(v):
        return v.reshape(mine, keep, -1)

    def flat(v):
        return v.reshape(rows, -1)

    def column_sums(v):
        return dot(jnp.ones((8, rows), BF), v, NN)[0]

    def normalize(v):
        center = jnp.mean(v, axis=-1, keepdims=True)
        var = jnp.mean(v * v, axis=-1, keepdims=True) - center * center
        scaled = lax.rsqrt(var + EPS)
        return (v - center) * scaled, scaled

    def norm_back(g, normed, scaled):
        a = jnp.mean(g, axis=-1, keepdims=True)
        b = jnp.mean(g * normed, axis=-1, keepdims=True)
        return (g - a - normed * b) * scaled

    normed_one, scaled_one = normalize(kept_slot)
    first_low = flat((normed_one * (1.0 + scale_one) + shift_one).astype(BF))
    first_low = step(first_low)
    w_as, qkvs, mixtures, wo_t = [], [], [], []
    attended = bias_wide[0]
    a_pairs = {0: (a_zc, a_yc)}
    for s in shifts:
        first, second = a_pairs[s]
        w_as.append(join((first[0], step(first[1])), (second[0], step(second[1]))))
        bias = jnp.concatenate(
            [bias_qv[s][0], jnp.zeros((own,), F32), bias_qv[s][1], jnp.zeros((own,), F32)]
        )
        qkv = step((dot(first_low, w_as[s], NN) + bias).astype(BF))
        qkvs.append(qkv)
        mixture = step(attend(own_counts, qkv, own, keep))
        mixtures.append(mixture)
        if s == 0:
            a_xys = later(a_xys)
            one_y = step(one_y)
            one_xs = [over_mp(one_z, t) for t in shifts]
            two_z = step(two_z)
            two_y = over_dp(two_z, 1)
            for t in shifts[1:]:
                a_pairs[t] = (core_pair(a_xs[t]), core_pair(a_xys[t]))
        wo_t.append(w_as[s][:, 3 * own :])
        attended = step(attended + dot(mixture, wo_t[s], NT))
    one_zc, one_yc = core_pair(one_z), core_pair(one_y)
    one_xs = later(one_xs)
    two_y = step(two_y)
    two_xs = [over_mp(two_z, s) for s in shifts]
    one_xys = [one_y, *[over_dp(v, 1) for v in one_xs[1:]]]
    g_one = {0: (one_zc, one_yc)}
    attended = cubes(attended)
    residual = kept_slot + gate_one * attended
    normed_two, scaled_two = normalize(residual)
    second_low = flat((normed_two * (1.0 + scale_two) + shift_two).astype(BF))
    second_low = step(second_low)
    g_two = {0: (core_pair(two_z), core_pair(two_y))}
    branch = bias_wide[1]
    w1, w2t, acts, slopes = [], [], [], []
    root = math.sqrt(2.0 / math.pi)
    for s in shifts:
        first, second = g_one[s]
        w1.append(join((first[0], step(first[1])), (second[0], step(second[1]))))
        hidden = dot(second_low, w1[s], NN) + bias_one[s]
        square = hidden * hidden
        bend = jnp.tanh(root * hidden * (1.0 + 0.044715 * square))
        act = (0.5 * hidden * (1.0 + bend)).astype(BF)
        slope = 0.5 * (1.0 + bend) + 0.5 * root * hidden * (1.0 - bend * bend) * (
            1.0 + 3.0 * 0.044715 * square
        )
        act, slope = step(act, slope)
        acts.append(act)
        slopes.append(slope)
        if s == 0:
            two_xs = later(two_xs)
            one_xys = later(one_xys)
            cols = ff // 384 * 128
            two_xys = [None]
            for t in shifts[1:]:
                two_xys.append(
                    (over_mp(two_y[:, :cols], t), over_dp(two_xs[t][:, cols:], 1))
                )
            for t in shifts[1:]:
                g_one[t] = (core_pair(one_xs[t]), core_pair(one_xys[t]))
            mixture_all = jnp.concatenate(mixtures, axis=1)
            cot_got = [over_mp(v, t) for t, v in enumerate(cot_parts)]
        if s == 1:
            for t in shifts[1:]:
                ends = [core_pair(step(v)) for v in two_xys[t]]
                g_two[t] = (core_pair(two_xs[t]), ends)
        first, second = g_two[s]
        if s:
            second = [(v[0], step(v[1])) for v in second]
            second = [jnp.concatenate([v[k] for v in second], axis=1) for k in range(2)]
            if s == 1:
                cot_got = later(cot_got)
        else:
            second = (second[0], step(second[1]))
        w2t.append(join((first[0], step(first[1])), second))
        branch = step(branch + dot(act, w2t[s], NT))
    branch = cubes(branch)
    result = residual + gate_two * branch
    result_low = flat(result).astype(BF)

    def add(a, b):
        return (a.astype(F32) + b.astype(F32)).astype(BF)

    near = zb * blk

    def keep_sum(low_side, v, got):
        return (dot(low_side, v, TN) + got.astype(F32)).astype(BF)

    def y_send(v):
        return over_dp(v[near:], 1)

    def y_add(v, got):
        return add(v[:near], got)

    def x_send(vs):
        return {s: over_mp(v, s) for s, v in vs.items() if s}

    def x_add(vs, got):
        total = vs[0].astype(F32)
        for v in got:
            total = total + v.astype(F32)
        return total.astype(BF)

    cot_rows = to_rows(cot_got).reshape(mine, keep, full)
    grad_result = cot_rows * own_scale
    grad_branch = flat((gate_two * grad_result).astype(BF))
    order = list(reversed(shifts))

    def far_scatter(v):
        v = v.reshape(zb * blk, -1)
        v = lax.psum_scatter(
            v, "dp", scatter_dimension=0, tiled=True, axis_index_groups=far_groups
        )
        return v

    low, high, grad_branch = step(grad_branch[:, :half], grad_branch[:, half:], grad_branch)
    two_got, two_kept, two_y_got, two_y, two_x_got = {}, {}, {}, {}, {}
    grad_hiddens = [None] * nm
    last = order[0]
    for s in order:
        two_got[s] = over_dp(step(dot(high, acts[s], TN, BF)), 0)
    for s in order:
        grad_hiddens[s] = step((dot(step(grad_branch), w2t[s], NN) * slopes[s]).astype(BF))
        two_kept[s] = step(keep_sum(low, acts[s], step(two_got[s])))
        two_y_got[s] = y_send(two_kept[s])
    low, high = step(second_low[:, :half], second_low[:, half:])
    one_got, one_kept, one_x_got = {}, {}, {}
    for s in order:
        one_got[s] = over_dp(step(dot(high, grad_hiddens[s], TN, BF)), 0)
    for s in order:
        one_kept[s] = step(keep_sum(low, grad_hiddens[s], step(one_got[s])))
        if s:
            one_x_got[s] = (over_mp(one_kept[s][near:], s), over_mp(one_kept[s][:near], s))
    grad_second = None
    for s in shifts:
        piece = dot(step(grad_hiddens[s]), w1[s], NT)
        grad_second = step(piece if grad_second is None else grad_second + piece)
    grad_second = cubes(step(grad_second))
    grad_shift_two = jnp.sum(grad_second, axis=1)
    grad_scale_two = jnp.sum(grad_second * normed_two, axis=1)
    grad_residual = grad_result + norm_back(
        grad_second * (1.0 + scale_two), normed_two, scaled_two
    )
    grad_attended = flat((gate_one * grad_residual).astype(BF))
    low, high, grad_attended = step(
        grad_attended[:, :half], grad_attended[:, half:], grad_attended
    )
    out_got = over_dp(step(dot(high, mixture_all, TN, BF)), 0)
    grad_mixtures = [step(dot(step(grad_attended), w, NN, BF)) for w in wo_t]
    for s in order[:-1]:
        two_y[s] = step(y_add(two_kept[s], step(two_y_got[s])))
        two_x_got[s] = over_mp(two_y[s], s)
    two_y[0] = step(y_add(two_kept[0], step(two_y_got[0])))
    one_high = step(x_add([one_kept[0][near:]], [step(v[0]) for v in one_x_got.values()]))
    one_y_got = over_dp(one_high, 1)
    out_kept = step(keep_sum(low, mixture_all, step(out_got)))
    out_y_got = y_send(out_kept)
    grad_qkvs, qkv_got, qk_kept, v_kept, qk_y_got, qk_y = [None] * nm, {}, {}, {}, {}, {}
    first_half, second_half = step(first_low[:, :half], first_low[:, half:])
    for s in order:
        grad_qkvs[s] = step(attend_back(step(own_counts), qkvs[s], grad_mixtures[s], keep))
        if s == last:
            one_x_got = {t: step(v[1]) for t, v in one_x_got.items()}
            one_low = step(x_add([one_kept[0][:near]], one_x_got.values()))
        else:
            one_y_got = step(one_y_got) if s == 0 else one_y_got
        qkv_got[s] = over_dp(step(dot(second_half, grad_qkvs[s], TN, BF)), 0)
    two_x = step(x_add(two_y, [step(v) for v in two_x_got.values()]))
    sum_two = far_scatter(two_x)
    one_y = step(add(one_low, one_y_got))
    fresh_got = from_rows(result_low)
    sum_one = far_scatter(one_y)
    v_x_got = {}
    for s in order:
        kept = step(keep_sum(first_half, grad_qkvs[s], step(qkv_got[s])))
        qk_kept[s], v_kept[s] = kept[:, : 2 * own], kept[:, 2 * own :]
        qk_y_got[s] = y_send(qk_kept[s])
        if s:
            v_x_got[s] = over_mp(v_kept[s], s)
    w_qkvs = [w[:, : 3 * own] for w in w_as]
    grad_first = step(dot(step(grad_qkvs[0]), w_qkvs[0], NT))
    for s in shifts[1:]:
        grad_first = step(grad_first + dot(step(grad_qkvs[s]), w_qkvs[s], NT))
    out_y = step(y_add(out_kept, step(out_y_got)))
    out_x_got = [over_mp(out_y[:, s * own : (s + 1) * own], s) for s in shifts[1:]]
    qk_y[last] = step(y_add(qk_kept[last], step(qk_y_got[last])))
    qk_x_got = {last: over_mp(qk_y[last], last)} if last else {}
    v_x = step(x_add(v_kept, [step(v) for v in v_x_got.values()]))
    v_y_got = y_send(v_x)
    grad_first = cubes(step(grad_first))
    grad_shift_one = jnp.sum(grad_first, axis=1)
    grad_scale_one = jnp.sum(grad_first * normed_one, axis=1)
    grad_gate_two = jnp.sum(grad_result * branch, axis=1)
    grad_gate_one = jnp.sum(grad_residual * attended, axis=1)
    grad_mod = jnp.stack(
        [
            grad_shift_one,
            grad_scale_one,
            grad_gate_one,
            grad_shift_two,
            grad_scale_two,
            grad_gate_two,
        ],
        axis=1,
    ).astype(BF)
    fresh_got = later(fresh_got)
    grad_mod = step(grad_mod.reshape(mine * 6, full))
    mod_back = [
        over_mp(dot(grad_mod, p, NT, BF).reshape(mine, 6 * own), s)
        for s, p in enumerate(spreads)
    ]
    if last:
        qk_x_got[last] = step(qk_x_got[last])
    out_x_got = [step(v) for v in out_x_got]
    for s in order[1:]:
        qk_y[s] = step(y_add(qk_kept[s], step(qk_y_got[s])))
        if s:
            qk_x_got[s] = over_mp(qk_y[s], s)
    mod_back = step(regroup(later(mod_back)))
    mod_gots = [over_far(mod_back, p) for p in range(1, zb)]
    out_x = x_add([out_y[:, :own]], out_x_got)
    qk_x = step(x_add(qk_y, [step(v) for v in qk_x_got.values()]))
    v_y = y_add(v_x, step(v_y_got))
    a_x = step(jnp.concatenate([qk_x, v_y, out_x], axis=1)).reshape(zb, blk, 4 * own)
    far_at = d >> 2
    far_kept = lax.dynamic_index_in_dim(a_x, far_at, 0, keepdims=False)
    far_sent = [
        lax.dynamic_index_in_dim(a_x, far_at ^ k, 0, keepdims=False) for k in range(1, zb)
    ]
    mod_gots = [step(v) for v in mod_gots]
    grad_mod_all = step(jnp.concatenate([mod_back, *mod_gots], 0))
    mod_got = over_dp(grad_mod_all, 1)
    far_got = [
        lax.ppermute(step(v), "dp", [(i, i ^ ((k + 1) << 2)) for i in range(nd)])
        for k, v in enumerate(far_sent)
    ]
    grad_kept = grad_residual + norm_back(
        step(grad_first) * (1.0 + scale_one), normed_one, scaled_one
    )
    grad_low = step(flat(grad_kept).astype(BF))
    grad_mod_all = step(jnp.concatenate([grad_mod_all, step(mod_got)], 0))
    mod_got = over_dp(grad_mod_all, 0)
    grad_got = from_rows(grad_low)
    grad_mod_all = step(jnp.concatenate([grad_mod_all, step(mod_got)], 0))
    grad_silu = dot(grad_mod_all, w_ada_flat, NT).reshape(nd, lat_dev * blk)
    grad_silu = exact_dot(place_hot.astype(F32), grad_silu, TN).reshape(nd, lat_dev, blk)
    grad_silu = lax.all_to_all(step(grad_silu), "dp", 0, 0)
    grad_attended, grad_branch, *held = step(
        grad_attended, grad_branch, *grad_qkvs, *grad_hiddens
    )
    grad_qkvs, grad_hiddens = held[:nm], held[nm:]
    bias_wide_sums = step(jnp.stack([column_sums(grad_attended), column_sums(grad_branch)]))
    grad_silu = step(grad_silu)
    grad_silu = jnp.swapaxes(grad_silu, 0, 1).reshape(lat_dev, nm, own)
    silu_got = [
        over_mp(lax.dynamic_index_in_dim(grad_silu, m ^ s, 1, keepdims=False), s) for s in shifts
    ]
    bias_own = 0.0
    for s in shifts:
        narrow = exact_dot(bias_wide_sums, spreads[s].astype(F32), NT)
        piece = jnp.concatenate(
            [
                column_sums(grad_qkvs[s][:, :own]),
                column_sums(grad_qkvs[s][:, 2 * own :]),
                column_sums(grad_hiddens[s]),
                narrow.reshape(-1),
            ]
        )
        bias_own = bias_own + step(over_mp(piece, s))
    far_got = [step(v) for v in far_got]
    bias_gots = [over_far(bias_own, p) for p in range(1, zb)]
    taken = jnp.sum(hot.astype(F32), axis=1)[:, None, :] > 0.5

    def put(got):
        return lax.dot_general(
            regroup(got), hot, (((1,), (1,)), ((0,), (0,))), preferred_element_type=F32
        )

    sum_ada = dot(silu_low, grad_mod_all, TN).reshape(blk, 6, own)
    grad_b_ada = jnp.sum(grad_mod_all.astype(F32), axis=0).reshape(6, own)
    sum_ada, grad_b_ada = step(sum_ada, grad_b_ada)
    input_grad = jnp.where(
        taken, put(later(grad_got)), cotangent.astype(F32) * row_scale[:, None, None]
    )
    input_grad = step(input_grad)
    for v in bias_gots:
        bias_own = bias_own + step(v)
    bias_got = over_dp(bias_own, 1)
    output = jnp.where(taken, put(fresh_got), inputs.astype(F32)).astype(BF)
    output = step(output)
    bias_own = step(bias_own + bias_got)
    bias_got = over_dp(bias_own, 0)
    sum_two, sum_one = step(sum_two, sum_one)
    sum_two, sum_one = sum_two.astype(F32), sum_one.astype(F32)
    total = far_kept.astype(F32)
    for v in far_got:
        total = total + v.astype(F32)
    total = step(total)
    bias_own = bias_own + bias_got
    cond_grad = jax.vjp(jax.nn.silu, condition.astype(F32))[1](sum(silu_got))[0]
    sum_qkv, sum_out = total[:, : 3 * own].reshape(blk, 3, own), total[:, 3 * own :]

    out_b_qv = bias_own[: 2 * own].reshape(2, own)
    out_b_one = bias_own[2 * own : 2 * own + ff]
    out_b_out = bias_own[2 * own + ff : 3 * own + ff]
    out_b_two = bias_own[3 * own + ff :]

    return (
        output,
        input_grad,
        cond_grad,
        sum_qkv,
        out_b_qv,
        sum_out.T,
        out_b_out,
        sum_one,
        out_b_one,
        sum_two.T,
        out_b_two,
        sum_ada,
        grad_b_ada,
    )


def solution(mesh):
    placed = (
        P("dp", "mp", None),
        P("dp", "mp"),
        P("dp", "mp", None),
        P("dp", None),
        P("dp"),
        P("dp"),
        P("dp", None, "mp"),
        P(None, "mp"),
        P("mp", "dp"),
        P("mp"),
        P("dp", "mp"),
        P("mp"),
        P("mp", "dp"),
        P("mp"),
        P("dp", None, "mp"),
        P(None, "mp"),
    )
    return jax.shard_map(
        local,
        mesh=mesh,
        in_specs=placed,
        out_specs=(
            P("dp", "mp", None),
            P("dp", "mp", None),
            P("dp", "mp"),
            P("dp", None, "mp"),
            P(None, "mp"),
            P("mp", "dp"),
            P("mp"),
            P("dp", "mp"),
            P("mp"),
            P("mp", "dp"),
            P("mp"),
            P("dp", None, "mp"),
            P(None, "mp"),
        ),
        check_vma=False,
    )
```

```python
from functools import partial
import math

import jax
import jax.numpy as jnp
from jax import lax
from jax.experimental import pallas as pl
from jax.experimental.pallas import tpu as pltpu
from jax.sharding import PartitionSpec as P

HD = 72
EPS = 1e-06
BF = jnp.bfloat16
F32 = jnp.float32
NN = ((1,), (0,))
NT = ((1,), (1,))
TN = ((0,), (0,))


def dot(left, right, dims, kind=F32):
    return lax.dot_general(left, right, (dims, ((), ())), preferred_element_type=kind)


def exact_dot(left, right, dims):
    return lax.dot_general(
        left,
        right,
        (dims, ((), ())),
        precision=lax.Precision.HIGHEST,
        preferred_element_type=F32,
    )


class Steps:
    def __init__(self):
        self.seen = ()

    def __call__(self, *values):
        out = lax.optimization_barrier((*values, *self.seen))[: len(values)]
        self.seen = out
        return out[0] if len(values) == 1 else out


def attend_kernel(heads, counts, qkv_ref, out_ref):
    count = counts[pl.program_id(0)]
    keep, own = out_ref.shape
    inv_root = 1.0 / math.sqrt(HD)
    valid = lax.broadcasted_iota(jnp.int32, (keep, keep), 1) < count
    for h in range(heads):
        a = HD * h
        q, k = qkv_ref[:, a : a + HD], qkv_ref[:, own + a : own + a + HD]
        v = qkv_ref[:, 2 * own + a : 2 * own + a + HD]
        scores = jnp.where(valid, dot(q, k, NT) * inv_root, -1e30)
        power = jnp.exp(scores - jnp.max(scores, axis=1, keepdims=True))
        probability = power / jnp.sum(power, axis=1, keepdims=True)
        out_ref[:, a : a + HD] = dot(probability.astype(BF), v, NN).astype(BF)


def attend_back_kernel(heads, counts, qkv_ref, g_ref, out_ref):
    count = counts[pl.program_id(0)]
    keep, own = g_ref.shape
    inv_root = 1.0 / math.sqrt(HD)
    valid = lax.broadcasted_iota(jnp.int32, (keep, keep), 0) < count
    for h in range(heads):
        a = HD * h
        q, k = qkv_ref[:, a : a + HD], qkv_ref[:, own + a : own + a + HD]
        v, g = qkv_ref[:, 2 * own + a : 2 * own + a + HD], g_ref[:, a : a + HD]
        scores = jnp.where(valid, dot(k, q, NT) * inv_root, -1e30)
        power = jnp.exp(scores - jnp.max(scores, axis=0, keepdims=True))
        probability = power / jnp.sum(power, axis=0, keepdims=True)
        grad_prob = dot(v, g, NT)
        delta = jnp.sum(grad_prob * probability, axis=0, keepdims=True)
        grad_scores = (probability * (grad_prob - delta)).astype(BF)
        out_ref[:, a : a + HD] = (dot(grad_scores, k, TN) * inv_root).astype(BF)
        out_ref[:, own + a : own + a + HD] = (dot(grad_scores, q, NN) * inv_root).astype(BF)
        out_ref[:, 2 * own + a : 2 * own + a + HD] = dot(probability.astype(BF), g, NN).astype(
            BF
        )


def attend(counts, qkv, own, keep):
    rows = qkv.shape[0]

    def block(n):
        return pl.BlockSpec((keep, n), lambda i, c: (i, 0))

    return pl.pallas_call(
        partial(attend_kernel, own // HD),
        out_shape=jax.ShapeDtypeStruct((rows, own), BF),
        grid_spec=pltpu.PrefetchScalarGridSpec(
            num_scalar_prefetch=1,
            grid=(rows // keep,),
            in_specs=[block(qkv.shape[1])],
            out_specs=block(own),
        ),
        compiler_params=pltpu.CompilerParams(vmem_limit_bytes=40 * 2**20),
    )(counts, qkv)


def attend_back(counts, qkv, g, keep):
    rows, own = g.shape

    def block(n):
        return pl.BlockSpec((keep, n), lambda i, c: (i, 0))

    return pl.pallas_call(
        partial(attend_back_kernel, own // HD),
        out_shape=jax.ShapeDtypeStruct((rows, 3 * own), BF),
        grid_spec=pltpu.PrefetchScalarGridSpec(
            num_scalar_prefetch=1,
            grid=(rows // keep,),
            in_specs=[block(qkv.shape[1]), block(own)],
            out_specs=block(3 * own),
        ),
        compiler_params=pltpu.CompilerParams(vmem_limit_bytes=40 * 2**20),
    )(counts, qkv, g)


def local(
    inputs,
    condition,
    cotangent,
    kept_rows,
    kept_counts,
    group_tokens,
    w_qkv,
    b_qv,
    w_out,
    b_out,
    w_one,
    b_one,
    w_two,
    b_two,
    w_ada,
    b_ada,
):
    nd, nm = lax.axis_size("dp"), lax.axis_size("mp")
    d, m = lax.axis_index("dp"), lax.axis_index("mp")
    lat_dev, own, seq = inputs.shape
    keep = kept_rows.shape[1]
    full = own * nm
    blk, nb = full // nd, nd // nm
    mine = lat_dev // nm
    rows = mine * keep
    ff = w_one.shape[1]
    half = full // 2
    far_bits = [b for b in reversed(range(2, nd.bit_length() - 1))]
    bits = far_bits + [1, 0]
    zb = 2 ** len(far_bits)
    shifts = range(nm)

    step = Steps()

    def over_dp(v, bit):
        return lax.ppermute(step(v), "dp", [(i, i ^ (1 << bit)) for i in range(nd)])

    def over_mp(v, s):
        if s == 0:
            return v
        return lax.ppermute(step(v), "mp", [(i, i ^ s) for i in range(nm)])

    def rel(place):
        out = jnp.zeros_like(place)
        for k, bit in enumerate(bits):
            out = out | (((place >> k) & 1) << bit)
        return out

    def block_of(place):
        near = place // zb
        return ((place % zb) << 2) | ((d & 3) ^ (((near & 1) << 1) | (near >> 1)))

    def spread(s, kind):
        place = lax.broadcasted_iota(jnp.int32, (own, full), 1)
        feature = lax.broadcasted_iota(jnp.int32, (own, full), 0)
        source = block_of(place // blk)
        wanted = (m ^ s) * nb + feature // blk
        return ((source == wanted) & (place % blk == feature % blk)).astype(kind)

    spreads = [spread(s, BF) for s in shifts]
    place_hot = (
        (d ^ rel(lax.broadcasted_iota(jnp.int32, (nd, nd), 0)))
        == lax.broadcasted_iota(jnp.int32, (nd, nd), 1)
    )
    far_groups = [[low + 4 * k for k in range(zb)] for low in range(4)]

    def group_of(v, s):
        return lax.dynamic_slice_in_dim(v, (m ^ s) * mine, mine, 0)

    def regroup(parts):
        stacked = jnp.stack(parts)
        return jnp.concatenate(
            [lax.dynamic_index_in_dim(stacked, m ^ g, 0, keepdims=False) for g in shifts]
        )

    def send_rows(v):
        return [over_mp(group_of(v, s), s).reshape(rows, own) for s in shifts]

    def to_rows(got):
        return sum(dot(g, p, NN) for g, p in zip(got, spreads))

    def from_rows(v):
        parts = [dot(v, p, NT, BF).reshape(mine, keep, own) for p in spreads]
        return [over_mp(part, s) for s, part in enumerate(parts)]

    def far_gather(v):
        return lax.all_gather(v, "dp", axis=0, tiled=True, axis_index_groups=far_groups)

    def later(vs):
        return [vs[0], *[step(v) for v in vs[1:]]]

    bias_vec = jnp.concatenate([b_qv.reshape(-1), b_one, b_out, b_two])
    bias_size = bias_vec.shape[0]
    bias_rows = -(-bias_size // own)
    bias_vec = jnp.pad(bias_vec, (0, bias_rows * own - bias_size)).reshape(bias_rows, own)
    small = jnp.concatenate([condition, bias_vec], axis=0)
    smalls = [over_mp(small, s) for s in shifts]
    w_a = jnp.concatenate([w_qkv.reshape(blk, 3 * own), w_out.T], axis=1)
    a_z = far_gather(w_a)
    one_z = far_gather(w_one)
    digits = jnp.stack([(group_tokens >> (8 * k)) & 255 for k in range(4)], axis=1)
    pad = -(blk + 4) % 8
    valid = jnp.arange(keep)[None, :] < kept_counts[:, None]
    hot = (
        (kept_rows[:, :, None] == jnp.arange(seq)[None, None, :]) & valid[:, :, None]
    ).astype(BF)

    def pick(source):
        return lax.dot_general(
            hot, source, (((2,), (2,)), ((0,), (0,))), preferred_element_type=BF
        )

    w_a, small = step(w_a, small)
    picked = step(pick(step(inputs)))
    kept_got = send_rows(picked)
    smalls = later(smalls)
    cond_halves = jnp.stack([v[:lat_dev] for v in smalls])
    bias_all = [v[lat_dev:].reshape(-1) for v in smalls]
    cond_full = jnp.concatenate(
        [lax.dynamic_index_in_dim(cond_halves, m ^ g, 0, keepdims=False) for g in shifts], axis=1
    )
    cond_send = step(
        jnp.concatenate(
            [
                jnp.swapaxes(cond_full.reshape(lat_dev, nd, blk), 0, 1),
                jnp.broadcast_to(digits.astype(BF)[None], (nd, lat_dev, 4)),
                jnp.zeros((nd, lat_dev, pad), BF),
            ],
            axis=2,
        )
    )
    cond_got = lax.all_to_all(cond_send, "dp", 0, 0)
    w_two_t = w_two.T
    w_ada_flat = w_ada.reshape(blk, 6 * own)
    two_z = far_gather(w_two_t)
    w_two_t, w_ada_flat, cond_got = step(w_two_t, w_ada_flat, cond_got)
    cond_got = dot(place_hot.astype(BF), cond_got.reshape(nd, -1), NN).reshape(
        nd, lat_dev, blk + 4 + pad
    )
    token_total = sum(
        jnp.sum(cond_got[:, :, blk + k]) * float(256**k) for k in range(4)
    )
    silu_low = jax.nn.silu(cond_got[:, :, :blk].reshape(nd * lat_dev, blk)).astype(BF)
    part = dot(silu_low, w_ada_flat, NN).reshape(nd, lat_dev, 6 * own)
    part = step(part)

    def part_send(part, bit):
        return over_dp(part[part.shape[0] // 2 :], bit)

    def part_add(part, got):
        return part[: part.shape[0] // 2] + got

    def far_mask(place):
        return sum(((place >> k) & 1) << bit for k, bit in enumerate(far_bits))

    def over_far(v, place):
        return lax.ppermute(step(v), "dp", [(i, i ^ far_mask(place)) for i in range(nd)])

    got = part_send(part, 0)
    part = part_add(part, step(got))
    got = part_send(part, 1)

    def core_pair(v):
        return (v, over_dp(v, 0))

    def join(first, second):
        return jnp.stack([first[0], second[0], first[1], second[1]]).reshape(full, -1)

    a_z = step(a_z)
    a_xs = [over_mp(a_z, s) for s in shifts]
    a_y = over_dp(a_z, 1)
    kept_got = later(kept_got)
    kept_slot = step(to_rows(kept_got)).reshape(mine, keep, full)
    part = step(part_add(part, step(got)))
    part_gots = [over_far(part[p], p) for p in range(1, zb)]
    a_zc = core_pair(a_z)
    cot_picked = step(pick(step(cotangent)))
    cot_parts = step(*[group_of(cot_picked, s).reshape(rows, own) for s in shifts])
    cot_parts = cot_parts if nm > 1 else [cot_parts]
    a_xs = later(a_xs)
    a_y = step(a_y)
    modulation = part[0] + b_ada.astype(F32).reshape(6 * own)
    for v in part_gots:
        modulation = modulation + step(v)
    modulation = step(modulation)

    def mod_group(s):
        own_part = group_of(modulation, s)
        return jnp.stack([own_part[:, k * own : (k + 1) * own] for k in range(6)]).reshape(
            6 * mine, own
        )

    mod_got = [over_mp(mod_group(s), s) for s in shifts]
    a_xys = [over_mp(a_y, s) for s in shifts]
    one_z = step(one_z)
    one_y = over_dp(one_z, 1)
    a_yc = core_pair(a_y)
    mod_got = later(mod_got)
    mod_rows = sum(
        exact_dot(v, p.astype(F32), NN) for v, p in zip(mod_got, spreads)
    ).reshape(6, mine, full)
    shift_one, scale_one, gate_one, shift_two, scale_two, gate_two = [
        mod_rows[k, :, None, :] for k in range(6)
    ]
    bias_qv = [v[: 2 * own].reshape(2, own).astype(F32) for v in bias_all]
    bias_one = [v[2 * own : 2 * own + ff].astype(F32) for v in bias_all]
    bias_wide = sum(
        dot(v[2 * own + ff : bias_size].reshape(2, own), p, NN) for v, p in zip(bias_all, spreads)
    )
    row_scale = lat_dev * nd * group_tokens.astype(F32) / token_total
    own_scale = group_of(row_scale, 0)[:, None, None]
    own_counts = group_of(kept_counts, 0)

    def cubes(v):
        return v.reshape(mine, keep, -1)

    def flat(v):
        return v.reshape(rows, -1)

    def column_sums(v):
        return dot(jnp.ones((8, rows), BF), v, NN)[0]

    def normalize(v):
        center = jnp.mean(v, axis=-1, keepdims=True)
        var = jnp.mean(v * v, axis=-1, keepdims=True) - center * center
        scaled = lax.rsqrt(var + EPS)
        return (v - center) * scaled, scaled

    def norm_back(g, normed, scaled):
        a = jnp.mean(g, axis=-1, keepdims=True)
        b = jnp.mean(g * normed, axis=-1, keepdims=True)
        return (g - a - normed * b) * scaled

    normed_one, scaled_one = normalize(kept_slot)
    first_low = flat((normed_one * (1.0 + scale_one) + shift_one).astype(BF))
    first_low = step(first_low)
    w_as, qkvs, mixtures, wo_t = [], [], [], []
    attended = bias_wide[0]
    a_pairs = {0: (a_zc, a_yc)}
    for s in shifts:
        first, second = a_pairs[s]
        w_as.append(join((first[0], step(first[1])), (second[0], step(second[1]))))
        bias = jnp.concatenate(
            [bias_qv[s][0], jnp.zeros((own,), F32), bias_qv[s][1], jnp.zeros((own,), F32)]
        )
        qkv = step((dot(first_low, w_as[s], NN) + bias).astype(BF))
        qkvs.append(qkv)
        mixture = step(attend(own_counts, qkv, own, keep))
        mixtures.append(mixture)
        if s == 0:
            a_xys = later(a_xys)
            one_y = step(one_y)
            one_xs = [over_mp(one_z, t) for t in shifts]
            two_z = step(two_z)
            two_y = over_dp(two_z, 1)
            for t in shifts[1:]:
                a_pairs[t] = (core_pair(a_xs[t]), core_pair(a_xys[t]))
        wo_t.append(w_as[s][:, 3 * own :])
        attended = step(attended + dot(mixture, wo_t[s], NT))
    one_zc, one_yc = core_pair(one_z), core_pair(one_y)
    one_xs = later(one_xs)
    two_y = step(two_y)
    two_xs = [over_mp(two_z, s) for s in shifts]
    one_xys = [one_y, *[over_dp(v, 1) for v in one_xs[1:]]]
    g_one = {0: (one_zc, one_yc)}
    attended = cubes(attended)
    residual = kept_slot + gate_one * attended
    normed_two, scaled_two = normalize(residual)
    second_low = flat((normed_two * (1.0 + scale_two) + shift_two).astype(BF))
    second_low = step(second_low)
    g_two = {0: (core_pair(two_z), core_pair(two_y))}
    branch = bias_wide[1]
    w1, w2t, acts, slopes = [], [], [], []
    root = math.sqrt(2.0 / math.pi)
    for s in shifts:
        first, second = g_one[s]
        w1.append(join((first[0], step(first[1])), (second[0], step(second[1]))))
        hidden = dot(second_low, w1[s], NN) + bias_one[s]
        square = hidden * hidden
        bend = jnp.tanh(root * hidden * (1.0 + 0.044715 * square))
        act = (0.5 * hidden * (1.0 + bend)).astype(BF)
        slope = 0.5 * (1.0 + bend) + 0.5 * root * hidden * (1.0 - bend * bend) * (
            1.0 + 3.0 * 0.044715 * square
        )
        act, slope = step(act, slope)
        acts.append(act)
        slopes.append(slope)
        if s == 0:
            two_xs = later(two_xs)
            one_xys = later(one_xys)
            cols = ff // 384 * 128
            two_xys = [None]
            for t in shifts[1:]:
                two_xys.append(
                    (over_mp(two_y[:, :cols], t), over_dp(two_xs[t][:, cols:], 1))
                )
            for t in shifts[1:]:
                g_one[t] = (core_pair(one_xs[t]), core_pair(one_xys[t]))
            mixture_all = jnp.concatenate(mixtures, axis=1)
            cot_got = [over_mp(v, t) for t, v in enumerate(cot_parts)]
        if s == 1:
            for t in shifts[1:]:
                ends = [core_pair(step(v)) for v in two_xys[t]]
                g_two[t] = (core_pair(two_xs[t]), ends)
        first, second = g_two[s]
        if s:
            second = [(v[0], step(v[1])) for v in second]
            second = [jnp.concatenate([v[k] for v in second], axis=1) for k in range(2)]
            if s == 1:
                cot_got = later(cot_got)
        else:
            second = (second[0], step(second[1]))
        w2t.append(join((first[0], step(first[1])), second))
        branch = step(branch + dot(act, w2t[s], NT))
    branch = cubes(branch)
    result = residual + gate_two * branch
    result_low = flat(result).astype(BF)

    def add(a, b):
        return (a.astype(F32) + b.astype(F32)).astype(BF)

    near = zb * blk

    def keep_sum(low_side, v, got):
        return (dot(low_side, v, TN) + got.astype(F32)).astype(BF)

    def y_send(v):
        return over_dp(v[near:], 1)

    def y_add(v, got):
        return add(v[:near], got)

    def x_send(vs):
        return {s: over_mp(v, s) for s, v in vs.items() if s}

    def x_add(vs, got):
        total = vs[0].astype(F32)
        for v in got:
            total = total + v.astype(F32)
        return total.astype(BF)

    cot_rows = to_rows(cot_got).reshape(mine, keep, full)
    grad_result = cot_rows * own_scale
    grad_branch = flat((gate_two * grad_result).astype(BF))
    order = list(reversed(shifts))

    def far_scatter(v):
        v = v.reshape(zb * blk, -1)
        v = lax.psum_scatter(
            v, "dp", scatter_dimension=0, tiled=True, axis_index_groups=far_groups
        )
        return v

    low, high, grad_branch = step(grad_branch[:, :half], grad_branch[:, half:], grad_branch)
    two_got, two_kept, two_y_got, two_y, two_x_got = {}, {}, {}, {}, {}
    grad_hiddens = [None] * nm
    last = order[0]
    for s in order:
        two_got[s] = over_dp(step(dot(high, acts[s], TN, BF)), 0)
    for s in order:
        grad_hiddens[s] = step((dot(step(grad_branch), w2t[s], NN) * slopes[s]).astype(BF))
        two_kept[s] = step(keep_sum(low, acts[s], step(two_got[s])))
        two_y_got[s] = y_send(two_kept[s])
    low, high = step(second_low[:, :half], second_low[:, half:])
    one_got, one_kept, one_x_got = {}, {}, {}
    for s in order:
        one_got[s] = over_dp(step(dot(high, grad_hiddens[s], TN, BF)), 0)
    for s in order:
        one_kept[s] = step(keep_sum(low, grad_hiddens[s], step(one_got[s])))
        if s:
            one_x_got[s] = (over_mp(one_kept[s][near:], s), over_mp(one_kept[s][:near], s))
    grad_second = None
    for s in shifts:
        piece = dot(step(grad_hiddens[s]), w1[s], NT)
        grad_second = step(piece if grad_second is None else grad_second + piece)
    grad_second = cubes(step(grad_second))
    grad_shift_two = jnp.sum(grad_second, axis=1)
    grad_scale_two = jnp.sum(grad_second * normed_two, axis=1)
    grad_residual = grad_result + norm_back(
        grad_second * (1.0 + scale_two), normed_two, scaled_two
    )
    grad_attended = flat((gate_one * grad_residual).astype(BF))
    low, high, grad_attended = step(
        grad_attended[:, :half], grad_attended[:, half:], grad_attended
    )
    out_got = over_dp(step(dot(high, mixture_all, TN, BF)), 0)
    grad_mixtures = [step(dot(step(grad_attended), w, NN, BF)) for w in wo_t]
    for s in order[:-1]:
        two_y[s] = step(y_add(two_kept[s], step(two_y_got[s])))
        two_x_got[s] = over_mp(two_y[s], s)
    two_y[0] = step(y_add(two_kept[0], step(two_y_got[0])))
    one_high = step(x_add([one_kept[0][near:]], [step(v[0]) for v in one_x_got.values()]))
    one_y_got = over_dp(one_high, 1)
    out_kept = step(keep_sum(low, mixture_all, step(out_got)))
    out_y_got = y_send(out_kept)
    grad_qkvs, qkv_got, qk_kept, v_kept, qk_y_got, qk_y = [None] * nm, {}, {}, {}, {}, {}
    first_half, second_half = step(first_low[:, :half], first_low[:, half:])
    for s in order:
        grad_qkvs[s] = step(attend_back(step(own_counts), qkvs[s], grad_mixtures[s], keep))
        if s == last:
            one_x_got = {t: step(v[1]) for t, v in one_x_got.items()}
            one_low = step(x_add([one_kept[0][:near]], one_x_got.values()))
        else:
            one_y_got = step(one_y_got) if s == 0 else one_y_got
        qkv_got[s] = over_dp(step(dot(second_half, grad_qkvs[s], TN, BF)), 0)
    two_x = step(x_add(two_y, [step(v) for v in two_x_got.values()]))
    sum_two = far_scatter(two_x)
    one_y = step(add(one_low, one_y_got))
    fresh_got = from_rows(result_low)
    sum_one = far_scatter(one_y)
    v_x_got = {}
    for s in order:
        kept = step(keep_sum(first_half, grad_qkvs[s], step(qkv_got[s])))
        qk_kept[s], v_kept[s] = kept[:, : 2 * own], kept[:, 2 * own :]
        qk_y_got[s] = y_send(qk_kept[s])
        if s:
            v_x_got[s] = over_mp(v_kept[s], s)
    w_qkvs = [w[:, : 3 * own] for w in w_as]
    grad_first = step(dot(step(grad_qkvs[0]), w_qkvs[0], NT))
    for s in shifts[1:]:
        grad_first = step(grad_first + dot(step(grad_qkvs[s]), w_qkvs[s], NT))
    out_y = step(y_add(out_kept, step(out_y_got)))
    out_x_got = [over_mp(out_y[:, s * own : (s + 1) * own], s) for s in shifts[1:]]
    qk_y[last] = step(y_add(qk_kept[last], step(qk_y_got[last])))
    qk_x_got = {last: over_mp(qk_y[last], last)} if last else {}
    grad_first = cubes(step(grad_first))
    grad_shift_one = jnp.sum(grad_first, axis=1)
    grad_scale_one = jnp.sum(grad_first * normed_one, axis=1)
    grad_gate_two = jnp.sum(grad_result * branch, axis=1)
    grad_gate_one = jnp.sum(grad_residual * attended, axis=1)
    grad_mod = jnp.stack(
        [
            grad_shift_one,
            grad_scale_one,
            grad_gate_one,
            grad_shift_two,
            grad_scale_two,
            grad_gate_two,
        ],
        axis=1,
    ).astype(BF)
    grad_mod = step(grad_mod.reshape(mine * 6, full))
    v_x = step(x_add(v_kept, [step(v) for v in v_x_got.values()]))
    v_y_got = y_send(v_x)
    fresh_got = later(fresh_got)
    mod_back = [
        over_mp(dot(grad_mod, p, NT, BF).reshape(mine, 6 * own), s)
        for s, p in enumerate(spreads)
    ]
    if last:
        qk_x_got[last] = step(qk_x_got[last])
    out_x_got = [step(v) for v in out_x_got]
    for s in order[1:]:
        qk_y[s] = step(y_add(qk_kept[s], step(qk_y_got[s])))
        if s:
            qk_x_got[s] = over_mp(qk_y[s], s)
    mod_back = step(regroup(later(mod_back)))
    mod_gots = [over_far(mod_back, p) for p in range(1, zb)]
    out_x = x_add([out_y[:, :own]], out_x_got)
    qk_x = step(x_add(qk_y, [step(v) for v in qk_x_got.values()]))
    v_y = y_add(v_x, step(v_y_got))
    a_x = step(jnp.concatenate([qk_x, v_y, out_x], axis=1)).reshape(zb, blk, 4 * own)
    far_at = d >> 2
    far_kept = lax.dynamic_index_in_dim(a_x, far_at, 0, keepdims=False)
    far_sent = [
        lax.dynamic_index_in_dim(a_x, far_at ^ k, 0, keepdims=False) for k in range(1, zb)
    ]
    mod_gots = [step(v) for v in mod_gots]
    grad_mod_all = step(jnp.concatenate([mod_back, *mod_gots], 0))
    mod_got = over_dp(grad_mod_all, 1)
    far_got = [
        lax.ppermute(step(v), "dp", [(i, i ^ ((k + 1) << 2)) for i in range(nd)])
        for k, v in enumerate(far_sent)
    ]
    grad_kept = grad_residual + norm_back(
        step(grad_first) * (1.0 + scale_one), normed_one, scaled_one
    )
    grad_low = step(flat(grad_kept).astype(BF))
    grad_mod_all = step(jnp.concatenate([grad_mod_all, step(mod_got)], 0))
    mod_got = over_dp(grad_mod_all, 0)
    grad_got = from_rows(grad_low)
    grad_mod_all = step(jnp.concatenate([grad_mod_all, step(mod_got)], 0))
    grad_silu = dot(grad_mod_all, w_ada_flat, NT).reshape(nd, lat_dev * blk)
    grad_silu = exact_dot(place_hot.astype(F32), grad_silu, TN).reshape(nd, lat_dev, blk)
    grad_silu = lax.all_to_all(step(grad_silu), "dp", 0, 0)
    grad_attended, grad_branch, *held = step(
        grad_attended, grad_branch, *grad_qkvs, *grad_hiddens
    )
    grad_qkvs, grad_hiddens = held[:nm], held[nm:]
    bias_wide_sums = step(jnp.stack([column_sums(grad_attended), column_sums(grad_branch)]))
    grad_silu = step(grad_silu)
    grad_silu = jnp.swapaxes(grad_silu, 0, 1).reshape(lat_dev, nm, own)
    silu_got = [
        over_mp(lax.dynamic_index_in_dim(grad_silu, m ^ s, 1, keepdims=False), s) for s in shifts
    ]
    bias_own = 0.0
    for s in shifts:
        narrow = exact_dot(bias_wide_sums, spreads[s].astype(F32), NT)
        piece = jnp.concatenate(
            [
                column_sums(grad_qkvs[s][:, :own]),
                column_sums(grad_qkvs[s][:, 2 * own :]),
                column_sums(grad_hiddens[s]),
                narrow.reshape(-1),
            ]
        )
        bias_own = bias_own + step(over_mp(piece, s))
    far_got = [step(v) for v in far_got]
    bias_gots = [over_far(bias_own, p) for p in range(1, zb)]
    taken = jnp.sum(hot.astype(F32), axis=1)[:, None, :] > 0.5

    def put(got):
        return lax.dot_general(
            regroup(got), hot, (((1,), (1,)), ((0,), (0,))), preferred_element_type=F32
        )

    sum_ada = dot(silu_low, grad_mod_all, TN).reshape(blk, 6, own)
    grad_b_ada = jnp.sum(grad_mod_all.astype(F32), axis=0).reshape(6, own)
    sum_ada, grad_b_ada = step(sum_ada, grad_b_ada)
    input_grad = jnp.where(
        taken, put(later(grad_got)), cotangent.astype(F32) * row_scale[:, None, None]
    )
    input_grad = step(input_grad)
    for v in bias_gots:
        bias_own = bias_own + step(v)
    bias_got = over_dp(bias_own, 1)
    output = jnp.where(taken, put([step(v) for v in fresh_got]), inputs.astype(F32)).astype(BF)
    output = step(output)
    bias_own = step(bias_own + bias_got)
    bias_got = over_dp(bias_own, 0)
    sum_two, sum_one = step(sum_two, sum_one)
    sum_two, sum_one = sum_two.astype(F32), sum_one.astype(F32)
    total = far_kept.astype(F32)
    for v in far_got:
        total = total + v.astype(F32)
    total = step(total)
    bias_own = bias_own + bias_got
    cond_grad = jax.vjp(jax.nn.silu, condition.astype(F32))[1](sum(silu_got))[0]
    sum_qkv, sum_out = total[:, : 3 * own].reshape(blk, 3, own), total[:, 3 * own :]

    out_b_qv = bias_own[: 2 * own].reshape(2, own)
    out_b_one = bias_own[2 * own : 2 * own + ff]
    out_b_out = bias_own[2 * own + ff : 3 * own + ff]
    out_b_two = bias_own[3 * own + ff :]

    return (
        output,
        input_grad,
        cond_grad,
        sum_qkv,
        out_b_qv,
        sum_out.T,
        out_b_out,
        sum_one,
        out_b_one,
        sum_two.T,
        out_b_two,
        sum_ada,
        grad_b_ada,
    )


def solution(mesh):
    placed = (
        P("dp", "mp", None),
        P("dp", "mp"),
        P("dp", "mp", None),
        P("dp", None),
        P("dp"),
        P("dp"),
        P("dp", None, "mp"),
        P(None, "mp"),
        P("mp", "dp"),
        P("mp"),
        P("dp", "mp"),
        P("mp"),
        P("mp", "dp"),
        P("mp"),
        P("dp", None, "mp"),
        P(None, "mp"),
    )
    return jax.shard_map(
        local,
        mesh=mesh,
        in_specs=placed,
        out_specs=(
            P("dp", "mp", None),
            P("dp", "mp", None),
            P("dp", "mp"),
            P("dp", None, "mp"),
            P(None, "mp"),
            P("mp", "dp"),
            P("mp"),
            P("dp", "mp"),
            P("mp"),
            P("mp", "dp"),
            P("mp"),
            P("dp", None, "mp"),
            P(None, "mp"),
        ),
        check_vma=False,
    )
```
